32 devices in a mesh: expert: 8 (over y, x, core), edata: 4 (over z).
Axes of the slice: x: 2, y: 2, z: 4, core: 2. Of those that a mesh axis runs over, the one named last changes fastest.
Arguments:
- out_grad: bfloat16 [16384, 4096], P(('expert', 'edata')), may hold values from -0.8984375 to 0.8984375
- hidden_saved: bfloat16 [16384, 768], P(('expert', 'edata')), may hold values from -6 to 6
- recv_counts: int32 [256], P(('expert', 'edata')), may hold values from 1 to 64, as said below
- master_weight: float32 [32768, 768], P(('expert', 'edata'))
- moment_one: bfloat16 [32768, 768], P(('expert', 'edata')), may hold values from -4 to 4
- moment_two: bfloat16 [32768, 768], P(('expert', 'edata')), may hold values from 0.049804688 to 0.5
Outputs:
- new_master: float32 [32768, 768], P(('expert', 'edata'))
- new_moment_one: bfloat16 [32768, 768], P(('expert', 'edata'))
- new_moment_two: bfloat16 [32768, 768], P(('expert', 'edata'))
- scaled_weight: bfloat16 [32768, 768], P('expert')
- expert_peak: float32 [8], P('expert')
The draws below stay inside these ranges and needn't reach their ends.
Inputs may be any that keep to these rules, and one draw needn't show every extreme that they name: `recv_counts`: counts are skewed over experts; in every draw some pair fills all 64 slots.
All inputs are finite; a program needn't handle non-finite values. Where the reference program divides by a largest or mean magnitude, that divisor is 1e-20 or more.
Results may differ from the reference program's by a relative error of at most 0.001.
Values may be sent and summed in bfloat16 or wider, within the bound.
No kernel may reach another device: no remote copies, remote signals or barrier semaphores. Data moves between devices by JAX's collectives and lax.ppermute only.
A program may use at most 128 MiB of HBM per device.

```python
import math
import jax
import jax.numpy as jnp
from jax import lax

D = 4096
FFN = 768
CAPACITY = 64
EXPERTS = 8
REPLICAS = 4


def draw_recv_counts(key, part):
    key_base = jax.random.fold_in(key, 11)
    key_heavy = jax.random.fold_in(key, 12)
    base = jax.random.randint(key_base, (EXPERTS, REPLICAS * EXPERTS), 1, CAPACITY + 1)
    heavy = jax.random.randint(key_heavy, (EXPERTS,), 0, 4) == 0
    counts = jnp.where(heavy[:, None], CAPACITY, base).reshape(-1).astype(jnp.int32)
    return counts.at[0].set(CAPACITY)


def draw_master_weight(key, part):
    rows = jnp.arange(EXPERTS * D) % D
    factor = 1.0 + 2.0 * rows.astype(jnp.float32) / float(max(D - 1, 1))
    values = jax.random.normal(key, (EXPERTS * D, FFN), jnp.float32)
    return (0.04 * values * factor[:, None]).astype(jnp.float32)


def with_spikes(entries, stream_key, source, target, blocks, factor):
    def block_of(axis_at):
        return (jnp.arange(entries.shape[axis_at]) // (entries.shape[axis_at] // blocks)).reshape((-1,) + (1,) * (entries.ndim - 1 - axis_at))

    near = jax.random.permutation(stream_key, blocks)[block_of(target)]
    far = (block_of(target) + blocks // 2) % blocks
    return jnp.where((block_of(source) == near) | (block_of(source) == far), factor * entries, entries)


def shard_levels(key, shape, cuts, smallest, largest):
    loudness, own = 1.0, jax.random.fold_in(key, 6)
    for axis_at, shards_of in cuts:
        heights = jnp.exp(jax.random.uniform(jax.random.fold_in(own, axis_at), (shards_of,), jnp.float32, smallest / len(cuts), largest / len(cuts)))
        loudness = loudness * jnp.repeat(heights, shape[axis_at] // shards_of).reshape([-1 if axis == axis_at else 1 for axis in range(len(shape))])
    return loudness


def noise(key, shape, scale, most, shards=(), dtype=jnp.bfloat16):
    loudness = shard_levels(key, shape, shards, -0.22, 0.18) if shards else 1.0
    values = jax.random.normal(key, shape, jnp.float32) * scale * loudness
    return jnp.minimum(jnp.maximum(values, -most), most).astype(dtype)


def gaussian_with(rng, shape, deviation, limit, pieces, heavy, kind=jnp.bfloat16):
    values = deviation * jax.random.normal(rng, shape, jnp.float32)
    if pieces:
        values = values * shard_levels(rng, shape, pieces, -0.22, 0.18)
    return jnp.clip(with_spikes(values, jax.random.fold_in(rng, 3), *heavy), -limit, limit).astype(kind)


def setup_inputs(seed: int = 0) -> dict:
    streams_of = jax.random.split(jax.random.key(seed), 7)
    out_grad = gaussian_with(streams_of[0], (REPLICAS * EXPERTS * EXPERTS * CAPACITY, D), 0.15, 0.8984375, ((0, 32),), (0, 1, 32, 2.75))
    hidden_saved = noise(streams_of[1], (EXPERTS * REPLICAS * EXPERTS * CAPACITY, FFN), 1.0, 6.0, ((0, 32),))
    recv_counts = draw_recv_counts(jax.random.fold_in(streams_of[6], 71), 0)
    master_weight = draw_master_weight(jax.random.fold_in(streams_of[6], 71), 0)
    moment_one = noise(streams_of[4], (EXPERTS * D, FFN), 1.0, 4.0, ((0, 32),))
    moment_two = jnp.clip(jnp.exp(math.log(0.5) - 2.306499 * jax.random.uniform(streams_of[5], (EXPERTS * D, FFN), jnp.float32) ** shard_levels(streams_of[5], (EXPERTS * D, FFN), ((0, 32),), -0.2, 0.2)), 0.049804688, 0.5).astype(jnp.bfloat16)
    return dict(out_grad=out_grad, hidden_saved=hidden_saved, recv_counts=recv_counts, master_weight=master_weight, moment_one=moment_one, moment_two=moment_two)


beta_one = 0.9
beta_two = 0.999
correct_one = 1.0 - 0.9 ** 5
correct_two = 1.0 - 0.999 ** 5
adam_eps = 1e-08
learn_rate = 0.05
weight_decay = 1.0
peak_eps = 1e-06

def reference(out_grad, hidden_saved, recv_counts, master_weight, moment_one, moment_two):
    grads_all = out_grad.reshape(EXPERTS, REPLICAS, EXPERTS, CAPACITY, D)
    hidden_all = hidden_saved.reshape(EXPERTS, REPLICAS, EXPERTS, CAPACITY, FFN)
    counts_all = recv_counts.reshape(EXPERTS, REPLICAS, EXPERTS)

    def one_expert(index):
        rows_in = lax.dynamic_index_in_dim(grads_all, index, 2, keepdims=False)
        rows_in = jnp.transpose(rows_in, (1, 0, 2, 3))
        hidden_in = lax.dynamic_index_in_dim(hidden_all, index, 0, keepdims=False)
        counts_in = lax.dynamic_index_in_dim(counts_all, index, 0, keepdims=False)
        slots = jnp.arange(CAPACITY).astype(jnp.int32)
        live = slots[None, None, :] < counts_in[:, :, None]
        masked = jnp.where(live[..., None], rows_in.astype(jnp.float32), jnp.float32(0.0))
        return jnp.einsum('rscd,rscf->df', masked, hidden_in.astype(jnp.float32))
    grad = lax.map(one_expert, jnp.arange(EXPERTS).astype(jnp.int32)).reshape(EXPERTS * D, FFN)
    first = beta_one * moment_one.astype(jnp.float32) + (1.0 - beta_one) * grad
    second = beta_two * moment_two.astype(jnp.float32) + (1.0 - beta_two) * grad * grad
    update = first / correct_one / (jnp.sqrt(second / correct_two) + adam_eps)
    new_master = master_weight - learn_rate * (update + weight_decay * master_weight)
    blocks = new_master.reshape(EXPERTS, D, FFN)
    expert_peak = lax.optimization_barrier(jnp.max(jnp.abs(blocks), axis=(1, 2)))
    scaled = (blocks / (expert_peak[:, None, None] + peak_eps)).astype(jnp.bfloat16)
    return (new_master, first.astype(jnp.bfloat16), second.astype(jnp.bfloat16), scaled.reshape(EXPERTS * D, FFN), expert_peak)
```

```python
import functools
import jax
import jax.numpy as jnp
from jax import lax
from jax.experimental import pallas as pl
from jax.experimental.pallas import tpu as pltpu
from jax.sharding import PartitionSpec as P

beta_one = 0.9
beta_two = 0.999
correct_one = 1.0 - 0.9**5
correct_two = 1.0 - 0.999**5
adam_eps = 1e-08
learn_rate = 0.05
weight_decay = 1.0
peak_eps = 1e-06

VMEM_LIMIT = 40 * 1024 * 1024
LEVELS = 32000.0
TAIL = 16


def params():
    return pltpu.CompilerParams(vmem_limit_bytes=VMEM_LIMIT)


def pick_kernel(table_ref, x_ref, o_ref):
    o_ref[...] = x_ref[...]


def pick_columns(x, starts, width):
    rows = x.shape[0]
    count = starts.shape[0]
    return pl.pallas_call(
        pick_kernel,
        out_shape=jax.ShapeDtypeStruct((rows, count * width), x.dtype),
        grid_spec=pltpu.PrefetchScalarGridSpec(
            num_scalar_prefetch=1,
            grid=(count, 2),
            in_specs=[pl.BlockSpec((rows // 2, width), lambda i, j, table: (j, table[i]))],
            out_specs=pl.BlockSpec((rows // 2, width), lambda i, j, table: (j, i)),
        ),
        compiler_params=params(),
        cost_estimate=pl.CostEstimate(
            flops=0, bytes_accessed=4 * rows * count * width, transcendentals=0
        ),
        name="pick_columns",
    )(starts, x)


def contract(rows_ref, hidden_ref):
    return lax.dot_general(
        rows_ref[...],
        hidden_ref[...],
        (((0,), (0,)), ((), ())),
        preferred_element_type=jnp.float32,
    )


def code_kernel(count, *refs):
    rows, hidden, out = refs[:count], refs[count : 2 * count], refs[2 * count]
    total = contract(rows[0], hidden[0])
    for k in range(1, count):
        total = total + contract(rows[k], hidden[k])
    block = total.shape[0]
    top = jnp.maximum(jnp.max(jnp.abs(total), axis=0, keepdims=True), 1e-30)
    exponent = jnp.floor(jnp.log2(top)) + 1.0
    step = jnp.exp2(exponent) * (1.0 / LEVELS)
    codes = jnp.round(total * (1.0 / step))
    out[0, :block, :] = codes.astype(jnp.int32).astype(jnp.int16)
    out[0, block:, :] = jnp.broadcast_to(
        exponent.astype(jnp.int32), (TAIL, total.shape[1])
    ).astype(jnp.int16)


def coded_sum(rows, offsets, hidden, width, block):
    count = len(rows)
    depth, ffn = hidden[0].shape
    blocks = width // block
    specs = [
        pl.BlockSpec((depth, block), functools.partial(lambda o, i: (0, o + i), off // block))
        for off in offsets
    ]
    return pl.pallas_call(
        functools.partial(code_kernel, count),
        out_shape=jax.ShapeDtypeStruct((blocks, block + TAIL, ffn), jnp.int16),
        grid=(blocks,),
        in_specs=specs + [pl.BlockSpec((depth, ffn), lambda i: (0, 0))] * count,
        out_specs=pl.BlockSpec((1, block + TAIL, ffn), lambda i: (i, 0, 0)),
        compiler_params=params(),
        cost_estimate=pl.CostEstimate(
            flops=2 * count * depth * width * ffn,
            bytes_accessed=2 * (count * depth * (width + ffn) + width * ffn),
            transcendentals=0,
        ),
        name="coded_sum",
    )(*rows, *hidden)


def adam_kernel(count, aliased, *refs):
    rows, hidden = refs[:count], refs[count : 2 * count]
    coded, master, one, two = refs[2 * count : 2 * count + 4]
    outs = refs[2 * count + 4 + aliased :]
    new_master_ref, new_one_ref, new_two_ref, top_ref = outs
    block = master.shape[0]
    step = jnp.exp2(coded[0, block : block + 1, :].astype(jnp.int32).astype(jnp.float32)) * (
        1.0 / LEVELS
    )
    grad = coded[0, :block, :].astype(jnp.int32).astype(jnp.float32) * step
    for k in range(count):
        grad = grad + contract(rows[k], hidden[k])
    first = beta_one * one[...].astype(jnp.float32) + (1.0 - beta_one) * grad
    second = beta_two * two[...].astype(jnp.float32) + (1.0 - beta_two) * grad * grad
    update = first / correct_one / (jnp.sqrt(second / correct_two) + adam_eps)
    weight = master[...]
    new_master = weight - learn_rate * (update + weight_decay * weight)
    new_master_ref[...] = new_master
    new_one_ref[...] = first.astype(jnp.bfloat16)
    new_two_ref[...] = second.astype(jnp.bfloat16)
    top = jnp.max(jnp.abs(new_master), axis=0, keepdims=True)

    @pl.when(pl.program_id(0) == 0)
    def _():
        top_ref[...] = top

    @pl.when(pl.program_id(0) > 0)
    def _():
        top_ref[...] = jnp.maximum(top_ref[...], top)


def adam(rows, offsets, hidden, coded, master, one, two, at, block, earlier=()):
    count = len(rows)
    depth, ffn = hidden[0].shape
    blocks = coded.shape[0]
    shard = master.shape[0]
    first_block = at // block
    specs = [
        pl.BlockSpec((depth, block), functools.partial(lambda o, i: (0, o + i), off // block))
        for off in offsets
    ]
    here = pl.BlockSpec((block, ffn), lambda i: (first_block + i, 0))
    whole = pl.BlockSpec(memory_space=pl.ANY)
    operands = 2 * count + 4
    return pl.pallas_call(
        functools.partial(adam_kernel, count, len(earlier)),
        out_shape=(
            jax.ShapeDtypeStruct((shard, ffn), jnp.float32),
            jax.ShapeDtypeStruct((shard, ffn), jnp.bfloat16),
            jax.ShapeDtypeStruct((shard, ffn), jnp.bfloat16),
            jax.ShapeDtypeStruct((1, ffn), jnp.float32),
        ),
        grid=(blocks,),
        in_specs=specs
        + [pl.BlockSpec((depth, ffn), lambda i: (0, 0))] * count
        + [pl.BlockSpec((1, block + TAIL, ffn), lambda i: (i, 0, 0)), here, here, here]
        + [whole] * len(earlier),
        out_specs=(here, here, here, pl.BlockSpec((1, ffn), lambda i: (0, 0))),
        input_output_aliases={operands + k: k for k in range(len(earlier))},
        compiler_params=params(),
        cost_estimate=pl.CostEstimate(
            flops=2 * count * depth * blocks * block * ffn,
            bytes_accessed=blocks * block * ffn * 18,
            transcendentals=0,
        ),
        name="adam",
    )(*rows, *hidden, coded, master, one, two, *earlier)


def local(out_grad, hidden_saved, recv_counts, master_weight, moment_one, moment_two):
    experts = lax.axis_size("expert")
    replicas = lax.axis_size("edata")
    me = lax.axis_index("edata")
    half = replicas // 2
    group = range(1, half)
    capacity = out_grad.shape[0] // experts
    shard = master_weight.shape[0]
    parts = 2
    width = shard // parts
    block = min(256, width)

    def swap(x, k):
        return lax.ppermute(x, "edata", [(i, i ^ k) for i in range(replicas)])

    live = (jnp.arange(capacity)[None, :] < recv_counts[:, None]).reshape(-1)
    hidden = jnp.where(live[:, None], hidden_saved, jnp.zeros((), jnp.bfloat16))
    hiddens = [hidden] + [swap(hidden, k) for k in group]

    def arrive(targets):
        starts = jnp.stack([d * parts + p for d, p in targets]).astype(jnp.int32)
        picked = pick_columns(out_grad, starts, width)
        return lax.all_to_all(picked, "expert", split_axis=0, concat_axis=0, tiled=True)

    coded = []
    for p in range(parts):
        got = arrive([(me ^ half ^ k, p) for k in range(half)])
        rows = [got] + [swap(got[:, k * width : (k + 1) * width], k) for k in group]
        coded.append(swap(coded_sum(rows, [0] * half, hiddens, width, block), half))

    results, tops = (), []
    got = arrive([(me ^ k, p) for k in range(half) for p in range(parts)])
    rows = [got] + [swap(got[:, k * shard : (k + 1) * shard], k) for k in group]
    for p in range(parts):
        *results, top = adam(
            rows,
            [p * width] * half,
            hiddens,
            coded[p],
            master_weight,
            moment_one,
            moment_two,
            p * width,
            block,
            tuple(results),
        )
        tops.append(top)
    new_master, new_one, new_two = results

    peak = functools.reduce(jnp.maximum, [jnp.max(top) for top in tops]).reshape(1)
    step = 1
    while step < replicas:
        peak = jnp.maximum(peak, swap(peak, step))
        step *= 2

    pieces = 2
    rows_of = shard // pieces
    own = [
        (new_master[i * rows_of : (i + 1) * rows_of] / (peak + peak_eps)).astype(jnp.bfloat16)
        for i in range(pieces)
    ]
    scaled = jnp.zeros((replicas * shard, new_master.shape[1]), jnp.bfloat16)

    def place(scaled, piece, source, i, valid=None):
        at = (source * shard + i * rows_of, 0)
        if valid is not None:
            piece = jnp.where(valid, piece, lax.dynamic_slice(scaled, at, piece.shape))
        return lax.dynamic_update_slice(scaled, piece, at)

    for i in range(pieces):
        scaled = place(scaled, own[i], me, i)
    down, up = list(own), list(own)
    for s in range(1, replicas):
        for i in range(pieces):
            down[i] = lax.ppermute(down[i], "edata", [(j, j - 1) for j in range(1, replicas)])
            up[i] = lax.ppermute(up[i], "edata", [(j, j + 1) for j in range(replicas - 1)])
        for i in range(pieces):
            scaled = place(scaled, down[i], jnp.minimum(me + s, replicas - 1), i, me + s < replicas)
            scaled = place(scaled, up[i], jnp.maximum(me - s, 0), i, me - s >= 0)
    return new_master, new_one, new_two, scaled, peak


def solution(mesh):
    placed = (
        P(("expert", "edata"), None),
        P(("expert", "edata"), None),
        P(("expert", "edata")),
        P(("expert", "edata"), None),
        P(("expert", "edata"), None),
        P(("expert", "edata"), None),
    )
    return jax.shard_map(
        local,
        mesh=mesh,
        in_specs=placed,
        out_specs=(
            P(("expert", "edata"), None),
            P(("expert", "edata"), None),
            P(("expert", "edata"), None),
            P("expert", None),
            P("expert"),
        ),
        check_vma=False,
    )
```

```python
import functools
import jax
import jax.numpy as jnp
from jax import lax
from jax.experimental import pallas as pl
from jax.experimental.pallas import tpu as pltpu
from jax.sharding import PartitionSpec as P

beta_one = 0.9
beta_two = 0.999
correct_one = 1.0 - 0.9**5
correct_two = 1.0 - 0.999**5
adam_eps = 1e-08
learn_rate = 0.05
weight_decay = 1.0
peak_eps = 1e-06

VMEM_LIMIT = 60 * 1024 * 1024
LEVELS = 32000.0
PLACE_HINT = 1 << 36
TAIL = 16


def params():
    return pltpu.CompilerParams(vmem_limit_bytes=VMEM_LIMIT)


def hint(amount):
    return pl.CostEstimate(flops=amount, bytes_accessed=amount, transcendentals=0)


def pick_kernel(strips, table_ref, x_ref, out_ref, buffer, sems_in, sems_out):
    rows = x_ref.shape[0]
    width = out_ref.shape[1]
    size = rows // strips
    moves = []
    for k in range(out_ref.shape[0] // size):
        i, j = divmod(k, strips)
        start = pl.multiple_of(table_ref[i] * width, width)
        there = pl.ds(k * size, size)
        moves.append(
            (
                pltpu.make_async_copy(
                    x_ref.at[pl.ds(j * size, size), pl.ds(start, width)],
                    buffer.at[there, :],
                    sems_in.at[k],
                ),
                pltpu.make_async_copy(buffer.at[there, :], out_ref.at[there, :], sems_out.at[k]),
            )
        )
    for come, _ in moves:
        come.start()
    for come, go in moves:
        come.wait()
        go.start()
    for _, go in moves:
        go.wait()


def pick_columns(x, chunks, width):
    rows, count, strips = x.shape[0], chunks.shape[0], 4
    anywhere = pl.BlockSpec(memory_space=pl.ANY)
    return pl.pallas_call(
        functools.partial(pick_kernel, strips),
        out_shape=jax.ShapeDtypeStruct((count * rows, width), x.dtype),
        in_specs=[pl.BlockSpec(memory_space=pltpu.SMEM), anywhere],
        out_specs=anywhere,
        scratch_shapes=[
            pltpu.VMEM((count * rows, width), x.dtype),
            pltpu.SemaphoreType.DMA((strips * count,)),
            pltpu.SemaphoreType.DMA((strips * count,)),
        ],
        compiler_params=params(),
        cost_estimate=hint(1024),
        name="pick_columns",
    )(chunks, x)


def gate_kernel(*refs):
    pass


def gate(x, after):
    if not after:
        return x
    anywhere = pl.BlockSpec(memory_space=pl.ANY)
    return pl.pallas_call(
        gate_kernel,
        out_shape=jax.ShapeDtypeStruct(x.shape, x.dtype),
        in_specs=[anywhere] * (1 + len(after)),
        out_specs=anywhere,
        input_output_aliases={0: 0},
        cost_estimate=hint(1024),
        name="gate",
    )(x, *after)


def contract(rows_ref, hidden_ref):
    return lax.dot_general(
        rows_ref[...],
        hidden_ref[...],
        (((0,), (0,)), ((), ())),
        preferred_element_type=jnp.float32,
    )


def group_sum(count, refs):
    rows, hidden = refs[1 : count + 1], refs[count + 1 : 2 * count + 1]
    total = contract(rows[0], hidden[0])
    for k in range(1, count):
        total = total + contract(rows[k], hidden[k])
    return total


def code_kernel(count, *refs):
    out = refs[-1]
    total = group_sum(count, refs)
    block = total.shape[0]
    top = jnp.maximum(jnp.max(jnp.abs(total), axis=0, keepdims=True), 1e-30)
    exponent = jnp.floor(jnp.log2(top)) + 1.0
    step = jnp.exp2(exponent) * (1.0 / LEVELS)
    codes = jnp.round(total * (1.0 / step))
    out[0, :block, :] = codes.astype(jnp.int32).astype(jnp.int16)
    out[0, block:, :] = jnp.broadcast_to(
        exponent.astype(jnp.int32), (TAIL, total.shape[1])
    ).astype(jnp.int16)


def sum_kernel(count, *refs):
    refs[-1][...] = group_sum(count, refs)


def summed(kernel, rows, order, hidden, at, width, block, out_shape, out_spec, name):
    count = len(hidden)
    depth, ffn = hidden[0].shape
    first = at // block
    return pl.pallas_call(
        functools.partial(kernel, count),
        out_shape=out_shape,
        grid_spec=pltpu.PrefetchScalarGridSpec(
            num_scalar_prefetch=1,
            grid=(width // block,),
            in_specs=[
                pl.BlockSpec(
                    (depth, block), functools.partial(lambda k, i, table: (table[k], first + i), k)
                )
                for k in range(count)
            ]
            + [pl.BlockSpec((depth, ffn), lambda i, table: (0, 0))] * count,
            out_specs=out_spec,
        ),
        compiler_params=params(),
        cost_estimate=hint(1024),
        name=name,
    )(order, *[rows] * count, *hidden)


def coded_sum(rows, order, hidden, at, width, block):
    ffn = hidden[0].shape[1]
    shape = jax.ShapeDtypeStruct((width // block, block + TAIL, ffn), jnp.int16)
    spec = pl.BlockSpec((1, block + TAIL, ffn), lambda i, table: (i, 0, 0))
    return summed(
        code_kernel, rows, order, hidden, at, width, block, shape, spec, "coded_sum"
    )


def own_sum(rows, order, hidden, block):
    ffn, width = hidden[0].shape[1], rows.shape[1]
    shape = jax.ShapeDtypeStruct((width, ffn), jnp.float32)
    spec = pl.BlockSpec((block, ffn), lambda i, table: (i, 0))
    return summed(sum_kernel, rows, order, hidden, 0, width, block, shape, spec, "own_sum")


def adam_kernel(arrays, at, block, size, *refs):
    streams = refs[:5]
    outs, top_ref = refs[-14:-11], refs[-11]
    buffers, results = refs[-10:-5], refs[-5:-2]
    arrived, left = refs[-2:]
    own, coded, master, one, two = buffers
    steps = coded.shape[0] * block // size
    comes, leaves = [], []
    for i in range(steps):
        here, there = pl.ds(i * size, size), pl.ds(at + i * size, size)
        pairs = [(x.at[there, :], y.at[here, :]) for x, y in zip(streams[2:], buffers[2:])]
        pairs.append((streams[0].at[there, :], own.at[here, :]))
        if i * size % block == 0:
            b = i * size // block
            pairs.append((streams[1].at[b], coded.at[b]))
        comes.append(
            [pltpu.make_async_copy(x, y, arrived.at[i, k]) for k, (x, y) in enumerate(pairs)]
        )
        leaves.append(
            [
                pltpu.make_async_copy(y.at[here, :], x.at[there, :], left.at[i, k])
                for k, (x, y) in enumerate(zip(outs, results))
            ]
        )
    for copies in comes:
        for copy in copies:
            copy.start()
    highest = None
    for i in range(steps):
        for copy in comes[i]:
            copy.wait()
        here = pl.ds(i * size, size)
        b, off = i * size // block, i * size % block
        exponent = coded[b, block : block + 1, :].astype(jnp.int32).astype(jnp.float32)
        codes = coded[b, off : off + size, :].astype(jnp.int32).astype(jnp.float32)
        grad = own[here, :] + codes * (jnp.exp2(exponent) * (1.0 / LEVELS))
        first = beta_one * one[here, :].astype(jnp.float32) + (1.0 - beta_one) * grad
        second = beta_two * two[here, :].astype(jnp.float32) + (1.0 - beta_two) * grad * grad
        update = (first * (1.0 / correct_one)) / (
            jnp.sqrt(second * (1.0 / correct_two)) + adam_eps
        )
        weight = master[here, :]
        new_master = weight - learn_rate * (update + weight_decay * weight)
        results[0][here, :] = new_master
        results[1][here, :] = first.astype(jnp.bfloat16)
        results[2][here, :] = second.astype(jnp.bfloat16)
        for copy in leaves[i]:
            copy.start()
        top = jnp.max(jnp.abs(new_master), axis=0, keepdims=True)
        highest = top if highest is None else jnp.maximum(highest, top)
    peak = jnp.max(highest)
    if arrays:
        peak = jnp.maximum(peak, refs[5 + arrays][0])
    top_ref[0] = peak
    for copies in leaves:
        for copy in copies:
            copy.wait()


def adam(own, coded, master, one, two, at, block, earlier=()):
    shard, ffn = master.shape
    size = min(128, block)
    width = coded.shape[0] * block
    steps = width // size
    anywhere = pl.BlockSpec(memory_space=pl.ANY)
    scalar = pl.BlockSpec(memory_space=pltpu.SMEM)
    arrays = max(len(earlier) - 1, 0)
    types = (jnp.float32, jnp.bfloat16, jnp.bfloat16)
    return pl.pallas_call(
        functools.partial(adam_kernel, arrays, at, block, size),
        out_shape=tuple(jax.ShapeDtypeStruct((shard, ffn), t) for t in types)
        + (jax.ShapeDtypeStruct((1,), jnp.float32),),
        in_specs=[anywhere] * (5 + arrays) + [scalar] * (arrays > 0),
        out_specs=(anywhere, anywhere, anywhere, scalar),
        scratch_shapes=[pltpu.VMEM((width, ffn), jnp.float32), pltpu.VMEM(coded.shape, jnp.int16)]
        + [pltpu.VMEM((width, ffn), t) for t in types * 2]
        + [pltpu.SemaphoreType.DMA((steps, 5)), pltpu.SemaphoreType.DMA((steps, 3))],
        input_output_aliases={5 + k: k for k in range(arrays)},
        compiler_params=params(),
        cost_estimate=hint(1024),
        name="adam",
    )(own, coded, master, one, two, *earlier)


def place_kernel(count, strips, table_ref, *refs):
    pieces = refs[:count]
    whole, buffer, sems_in, sems_out = refs[-4:]
    rows = pieces[0].shape[0]
    size = rows // strips

    def come(k, j):
        strip = pl.ds(j * size, size)
        return pltpu.make_async_copy(
            pieces[k].at[strip, :], buffer.at[k, strip, :], sems_in.at[k, j]
        )

    def leave(k, j):
        at = pl.multiple_of(table_ref[2 * k] * rows + j * size, size)
        return pltpu.make_async_copy(
            buffer.at[k, pl.ds(j * size, size), :], whole.at[pl.ds(at, size), :], sems_out.at[k, j]
        )

    for k in range(count):

        @pl.when(table_ref[2 * k + 1] > 0)
        def _():
            for j in range(strips):
                come(k, j).start()

    for k in range(count):

        @pl.when(table_ref[2 * k + 1] > 0)
        def _():
            for j in range(strips):
                come(k, j).wait()
                leave(k, j).start()

    for k in range(count):

        @pl.when(table_ref[2 * k + 1] > 0)
        def _():
            for j in range(strips):
                leave(k, j).wait()


def place(whole, shape, pieces, spots):
    count, strips = len(pieces), 4
    table = jnp.stack([jnp.asarray(v).astype(jnp.int32) for spot in spots for v in spot])
    anywhere = pl.BlockSpec(memory_space=pl.ANY)
    earlier = () if whole is None else (whole,)
    return pl.pallas_call(
        functools.partial(place_kernel, count, strips),
        out_shape=jax.ShapeDtypeStruct(shape, jnp.bfloat16),
        in_specs=[pl.BlockSpec(memory_space=pltpu.SMEM)] + [anywhere] * (count + len(earlier)),
        out_specs=anywhere,
        scratch_shapes=[
            pltpu.VMEM((count,) + pieces[0].shape, jnp.bfloat16),
            pltpu.SemaphoreType.DMA((count, strips)),
            pltpu.SemaphoreType.DMA((count, strips)),
        ],
        input_output_aliases={1 + count: 0} if earlier else {},
        compiler_params=params(),
        cost_estimate=hint(PLACE_HINT),
        name="place",
    )(table, *pieces, *earlier)


def local(out_grad, hidden_saved, recv_counts, master_weight, moment_one, moment_two):
    experts = lax.axis_size("expert")
    half = lax.axis_size("near")
    replicas = lax.axis_size("far") * half
    near, far = lax.axis_index("near"), lax.axis_index("far")
    me = far * half + near
    capacity = out_grad.shape[0] // experts
    shard, ffn = master_weight.shape
    block = min(256, shard // 2)
    chain = ("far", "near")

    def swap(x, k):
        return lax.ppermute(x, chain, [(i, i ^ k) for i in range(replicas)])

    live = (jnp.arange(capacity)[None, :] < recv_counts[:, None]).reshape(-1)
    hidden = jnp.where(live[:, None], hidden_saved, jnp.zeros((), jnp.bfloat16))
    hiddens = [hidden] + [swap(hidden, k) for k in range(1, half)]
    order = jnp.stack([near ^ k for k in range(half)]).astype(jnp.int32)

    def arrive(side, after):
        chunks = (side * half + jnp.arange(half)).astype(jnp.int32)
        picked = gate(pick_columns(out_grad, chunks, shard), after)
        return lax.all_to_all(picked, ("near", "expert"), 0, 0, tiled=True)

    part = shard // 2
    got = arrive(1 - far, ())
    partials = [coded_sum(got, order, hiddens, p * part, part, block) for p in range(2)]
    coded = [swap(partial, half) for partial in partials]

    got = arrive(far, (partials[0],))
    own = own_sum(got, order, hiddens, block)
    results = ()
    for p in range(2):
        results = adam(
            own, coded[p], master_weight, moment_one, moment_two, p * part, block, tuple(results)
        )
    new_master, new_one, new_two, peak = results

    step = 1
    while step < replicas:
        peak = jnp.maximum(peak, swap(peak, step))
        step *= 2

    pieces = 2
    size = shard // pieces
    whole_shape = (replicas * shard, ffn)
    inverse = 1.0 / (peak + peak_eps)
    down = [
        (new_master[i * size : (i + 1) * size] * inverse).astype(jnp.bfloat16)
        for i in range(pieces)
    ]
    up = list(down)
    scaled = place(None, whole_shape, down, [(me * pieces + i, 1) for i in range(pieces)])
    for s in range(1, replicas):
        for i in range(pieces):
            down[i] = lax.ppermute(down[i], chain, [(j, j - 1) for j in range(1, replicas)])
            up[i] = lax.ppermute(up[i], chain, [(j, j + 1) for j in range(replicas - 1)])
        for i in range(pieces):
            scaled = place(
                scaled,
                whole_shape,
                [down[i], up[i]],
                [
                    (jnp.minimum(me + s, replicas - 1) * pieces + i, me + s < replicas),
                    (jnp.maximum(me - s, 0) * pieces + i, me >= s),
                ],
            )
    return new_master, new_one, new_two, scaled, peak


def solution(mesh):
    experts, replicas = mesh.devices.shape
    cut = jax.sharding.Mesh(
        mesh.devices.reshape(experts, 2, replicas // 2), ("expert", "far", "near")
    )
    everything = ("expert", "far", "near")
    placed = P(everything, None)
    return jax.shard_map(
        local,
        mesh=cut,
        in_specs=(placed, placed, P(everything), placed, placed, placed),
        out_specs=(placed, placed, placed, P("expert", None), P("expert")),
        check_vma=False,
    )
```

```python
import functools
import jax
import jax.numpy as jnp
from jax import lax
from jax.experimental import pallas as pl
from jax.experimental.pallas import tpu as pltpu
from jax.sharding import PartitionSpec as P

beta_one = 0.9
beta_two = 0.999
correct_one = 1.0 - 0.9**5
correct_two = 1.0 - 0.999**5
adam_eps = 1e-08
learn_rate = 0.05
weight_decay = 1.0
peak_eps = 1e-06

MIB = 1024 * 1024
LEVELS = 32000.0
PLACE_HINT = 1 << 32
TAIL = 16


def params(mib=24):
    return pltpu.CompilerParams(vmem_limit_bytes=mib * MIB)


def hint(amount):
    return pl.CostEstimate(flops=amount, bytes_accessed=amount, transcendentals=0)


def pick_kernel(strips, table_ref, x_ref, out_ref, buffer, sems_in, sems_out):
    rows = x_ref.shape[0]
    width = out_ref.shape[1]
    size = rows // strips
    moves = []
    for k in range(out_ref.shape[0] // size):
        i, j = divmod(k, strips)
        start = pl.multiple_of(table_ref[i] * width, width)
        there = pl.ds(k * size, size)
        moves.append(
            (
                pltpu.make_async_copy(
                    x_ref.at[pl.ds(j * size, size), pl.ds(start, width)],
                    buffer.at[there, :],
                    sems_in.at[k],
                ),
                pltpu.make_async_copy(buffer.at[there, :], out_ref.at[there, :], sems_out.at[k]),
            )
        )
    for come, _ in moves:
        come.start()
    for come, go in moves:
        come.wait()
        go.start()
    for _, go in moves:
        go.wait()


def pick_columns(x, chunks, width):
    rows, count, strips = x.shape[0], chunks.shape[0], 4
    anywhere = pl.BlockSpec(memory_space=pl.ANY)
    return pl.pallas_call(
        functools.partial(pick_kernel, strips),
        out_shape=jax.ShapeDtypeStruct((count * rows, width), x.dtype),
        in_specs=[pl.BlockSpec(memory_space=pltpu.SMEM), anywhere],
        out_specs=anywhere,
        scratch_shapes=[
            pltpu.VMEM((count * rows, width), x.dtype),
            pltpu.SemaphoreType.DMA((strips * count,)),
            pltpu.SemaphoreType.DMA((strips * count,)),
        ],
        compiler_params=params(60),
        cost_estimate=hint(1024),
        name="pick_columns",
    )(chunks, x)


def gate_kernel(*refs):
    pass


def gate(x, after):
    if not after:
        return x
    anywhere = pl.BlockSpec(memory_space=pl.ANY)
    return pl.pallas_call(
        gate_kernel,
        out_shape=jax.ShapeDtypeStruct(x.shape, x.dtype),
        in_specs=[anywhere] * (1 + len(after)),
        out_specs=anywhere,
        input_output_aliases={0: 0},
        cost_estimate=hint(1024),
        name="gate",
    )(x, *after)


def contract(rows_ref, hidden_ref):
    return lax.dot_general(
        rows_ref[...],
        hidden_ref[...],
        (((0,), (0,)), ((), ())),
        preferred_element_type=jnp.float32,
    )


def group_sum(count, refs):
    rows, hidden = refs[1 : count + 1], refs[count + 1 : 2 * count + 1]
    total = contract(rows[0], hidden[0])
    for k in range(1, count):
        total = total + contract(rows[k], hidden[k])
    return total


def encode(values, out):
    block = values.shape[0]
    top = jnp.maximum(jnp.max(jnp.abs(values), axis=0, keepdims=True), 1e-30)
    exponent = jnp.floor(jnp.log2(top)) + 1.0
    codes = jnp.round(values * (1.0 / (jnp.exp2(exponent) * (1.0 / LEVELS))))
    out[:block, :] = codes.astype(jnp.int32).astype(jnp.int16)
    out[block:, :] = jnp.broadcast_to(
        exponent.astype(jnp.int32), (TAIL, values.shape[1])
    ).astype(jnp.int16)


def decode(coded, rows):
    block = coded.shape[0] - TAIL
    exponent = coded[block : block + 1, :].astype(jnp.int32).astype(jnp.float32)
    codes = coded[rows, :].astype(jnp.int32).astype(jnp.float32)
    return codes * (jnp.exp2(exponent) * (1.0 / LEVELS))


def code_kernel(count, *refs):
    encode(group_sum(count, refs), refs[-1].at[0])


def sum_kernel(count, *refs):
    refs[-1][...] = group_sum(count, refs)


def summed(kernel, rows, order, hidden, at, width, block, out_shape, out_spec, name):
    count = len(hidden)
    depth, ffn = hidden[0].shape
    first = at // block
    return pl.pallas_call(
        functools.partial(kernel, count),
        out_shape=out_shape,
        grid_spec=pltpu.PrefetchScalarGridSpec(
            num_scalar_prefetch=1,
            grid=(width // block,),
            in_specs=[
                pl.BlockSpec(
                    (depth, block), functools.partial(lambda k, i, table: (table[k], first + i), k)
                )
                for k in range(count)
            ]
            + [pl.BlockSpec((depth, ffn), lambda i, table: (0, 0))] * count,
            out_specs=out_spec,
        ),
        compiler_params=params(),
        cost_estimate=hint(1024),
        name=name,
    )(order, *[rows] * count, *hidden)


def coded_sum(rows, order, hidden, at, width, block):
    ffn = hidden[0].shape[1]
    shape = jax.ShapeDtypeStruct((width // block, block + TAIL, ffn), jnp.int16)
    spec = pl.BlockSpec((1, block + TAIL, ffn), lambda i, table: (i, 0, 0))
    return summed(
        code_kernel, rows, order, hidden, at, width, block, shape, spec, "coded_sum"
    )


def own_sum(rows, order, hidden, block):
    ffn, width = hidden[0].shape[1], rows.shape[1]
    shape = jax.ShapeDtypeStruct((width, ffn), jnp.float32)
    spec = pl.BlockSpec((block, ffn), lambda i, table: (i, 0))
    return summed(sum_kernel, rows, order, hidden, 0, width, block, shape, spec, "own_sum")


def adam_kernel(arrays, at, block, size, ahead, *refs):
    streams = refs[:5]
    refs, (early,) = (refs[:-11] + refs[-10:], refs[-11:-10]) if ahead else (refs, (None,))
    outs, top_ref = refs[-14:-11], refs[-11]
    buffers, results = refs[-10:-5], refs[-5:-2]
    arrived, left = refs[-2:]
    own, coded, master, one, two = buffers
    steps = coded.shape[0] * block // size
    comes, leaves = [], []
    for i in range(steps):
        here, there = pl.ds(i * size, size), pl.ds(at + i * size, size)
        pairs = [(x.at[there, :], y.at[here, :]) for x, y in zip(streams[2:], buffers[2:])]
        pairs.append((streams[0].at[there, :], own.at[here, :]))
        if i * size % block == 0:
            b = i * size // block
            pairs.append((streams[1].at[b], coded.at[b]))
        comes.append(
            [pltpu.make_async_copy(x, y, arrived.at[i, k]) for k, (x, y) in enumerate(pairs)]
        )
        leaves.append(
            [
                pltpu.make_async_copy(y.at[here, :], x.at[there, :], left.at[i, k])
                for k, (x, y) in enumerate(zip(outs, results))
            ]
        )
    for copies in comes:
        for copy in copies:
            copy.start()
    highest = None
    for i in range(steps):
        for copy in comes[i]:
            copy.wait()
        here = pl.ds(i * size, size)
        b, off = i * size // block, i * size % block
        grad = own[here, :] + decode(coded.at[b], pl.ds(off, size))
        first = beta_one * one[here, :].astype(jnp.float32) + (1.0 - beta_one) * grad
        second = beta_two * two[here, :].astype(jnp.float32) + (1.0 - beta_two) * grad * grad
        update = (first * (1.0 / correct_one)) / (
            jnp.sqrt(second * (1.0 / correct_two)) + adam_eps
        )
        weight = master[here, :]
        new_master = weight - learn_rate * (update + weight_decay * weight)
        results[0][here, :] = new_master
        results[1][here, :] = first.astype(jnp.bfloat16)
        results[2][here, :] = second.astype(jnp.bfloat16)
        for copy in leaves[i]:
            copy.start()
        top = jnp.max(jnp.abs(new_master), axis=0, keepdims=True)
        highest = top if highest is None else jnp.maximum(highest, top)
        if ahead and off + size == block:
            encode(results[0][pl.ds(b * block, block), :], early.at[b])
    peak = jnp.max(highest)
    if arrays:
        peak = jnp.maximum(peak, refs[5 + arrays][0])
    top_ref[0] = peak
    for copies in leaves:
        for copy in copies:
            copy.wait()


def adam(own, coded, master, one, two, at, block, ahead, earlier=()):
    shard, ffn = master.shape
    size = min(128, block)
    width = coded.shape[0] * block
    steps = width // size
    anywhere = pl.BlockSpec(memory_space=pl.ANY)
    scalar = pl.BlockSpec(memory_space=pltpu.SMEM)
    arrays = max(len(earlier) - 1, 0)
    types = (jnp.float32, jnp.bfloat16, jnp.bfloat16)
    return pl.pallas_call(
        functools.partial(adam_kernel, arrays, at, block, size, ahead),
        out_shape=tuple(jax.ShapeDtypeStruct((shard, ffn), t) for t in types)
        + (jax.ShapeDtypeStruct((1,), jnp.float32),)
        + (jax.ShapeDtypeStruct(coded.shape, jnp.int16),) * ahead,
        in_specs=[anywhere] * (5 + arrays) + [scalar] * (arrays > 0),
        out_specs=(anywhere, anywhere, anywhere, scalar)
        + (pl.BlockSpec(memory_space=pltpu.VMEM),) * ahead,
        scratch_shapes=[pltpu.VMEM((width, ffn), jnp.float32), pltpu.VMEM(coded.shape, jnp.int16)]
        + [pltpu.VMEM((width, ffn), t) for t in types * 2]
        + [pltpu.SemaphoreType.DMA((steps, 5)), pltpu.SemaphoreType.DMA((steps, 3))],
        input_output_aliases={5 + k: k for k in range(arrays)},
        compiler_params=params(60),
        cost_estimate=hint(1024),
        name="adam",
    )(own, coded, master, one, two, *earlier)


def scale_kernel(peak_ref, weight_ref, *refs):
    out_ref = refs[-1]
    factor = 1.0 / (jnp.full((1, out_ref.shape[1]), peak_ref[0], jnp.float32) + peak_eps)
    out_ref[...] = (weight_ref[...] * factor).astype(jnp.bfloat16)


def scale(weight, peak, at, rows, after):
    ffn = weight.shape[1]
    block = rows // 2
    return pl.pallas_call(
        scale_kernel,
        out_shape=jax.ShapeDtypeStruct((rows, ffn), jnp.bfloat16),
        grid=(2,),
        in_specs=[
            pl.BlockSpec(memory_space=pltpu.SMEM),
            pl.BlockSpec((block, ffn), lambda i: (at // block + i, 0)),
        ]
        + [pl.BlockSpec(memory_space=pl.ANY)] * len(after),
        out_specs=pl.BlockSpec((block, ffn), lambda i: (i, 0)),
        compiler_params=params(),
        cost_estimate=hint(1024),
        name="scale",
    )(peak, weight, *after)


def place_kernel(strips, coded, table_ref, factor_ref, piece, *refs):
    whole, landed, scaled, sems_in, sems_out = refs[-5:]
    rows = scaled.shape[0]
    size = rows // strips
    at = pl.multiple_of(table_ref[0] * rows, rows)
    comes, leaves = [], []
    for j in range(strips):
        here = pl.ds(j * size, size)
        comes.append(
            pltpu.make_async_copy(piece.at[here, :], landed.at[here, :], sems_in.at[j])
        )
        leaves.append(
            pltpu.make_async_copy(
                (scaled if coded else landed).at[here, :],
                whole.at[pl.ds(at + j * size, size), :],
                sems_out.at[j],
            )
        )
    if coded:
        last = pl.ds(rows, TAIL)
        comes.append(
            pltpu.make_async_copy(piece.at[last, :], landed.at[last, :], sems_in.at[strips])
        )
    for copy in comes:
        copy.start()
    if coded:
        comes[-1].wait()
    for j in range(strips):
        comes[j].wait()
        if coded:
            here = pl.ds(j * size, size)
            values = decode(landed, here) * factor_ref[0]
            scaled[here, :] = values.astype(jnp.bfloat16)
        leaves[j].start()
    for copy in leaves:
        copy.wait()


def place(whole, shape, piece, spot, factor):
    coded = piece.dtype == jnp.int16
    rows, ffn = piece.shape
    rows -= TAIL * coded
    strips = 4
    anywhere = pl.BlockSpec(memory_space=pl.ANY)
    scalars = pl.BlockSpec(memory_space=pltpu.SMEM)
    earlier = () if whole is None else (whole,)
    return pl.pallas_call(
        functools.partial(place_kernel, strips, coded),
        out_shape=jax.ShapeDtypeStruct(shape, jnp.bfloat16),
        in_specs=[scalars, scalars, anywhere] + [anywhere] * len(earlier),
        out_specs=anywhere,
        scratch_shapes=[
            pltpu.VMEM(piece.shape, piece.dtype),
            pltpu.VMEM((rows, ffn), jnp.bfloat16),
            pltpu.SemaphoreType.DMA((strips + 1,)),
            pltpu.SemaphoreType.DMA((strips,)),
        ],
        input_output_aliases={3: 0} if earlier else {},
        compiler_params=params(),
        cost_estimate=hint(PLACE_HINT),
        name="place",
    )(spot.astype(jnp.int32).reshape(1), factor, piece, *earlier)


def local(out_grad, hidden_saved, recv_counts, master_weight, moment_one, moment_two):
    experts = lax.axis_size("expert")
    half = lax.axis_size("near")
    replicas = lax.axis_size("far") * half
    near, far = lax.axis_index("near"), lax.axis_index("far")
    me = far * half + near
    capacity = out_grad.shape[0] // experts
    shard, ffn = master_weight.shape
    block, part = min(256, shard // 2), shard // 2
    chain = ("far", "near")

    def swap(x, k):
        return lax.ppermute(x, chain, [(i, i ^ k) for i in range(replicas)])

    live = (jnp.arange(capacity)[None, :] < recv_counts[:, None]).reshape(-1)
    hidden = jnp.where(live[:, None], hidden_saved, jnp.zeros((), jnp.bfloat16))
    hiddens = [hidden] + [swap(hidden, k) for k in range(1, half)]
    order = jnp.stack([near ^ k for k in range(half)]).astype(jnp.int32)

    def arrive(side, at, width, after):
        chunks = ((side * half + jnp.arange(half)) * shard + at) // width
        picked = gate(pick_columns(out_grad, chunks.astype(jnp.int32), width), after)
        return lax.all_to_all(picked, ("near", "expert"), 0, 0, tiled=True)

    got = arrive(1 - far, 0, shard, ())
    partials = [
        coded_sum(got, order, hiddens, at, block, block) for at in range(0, shard, block)
    ]
    coded = [swap(partial, half) for partial in partials]

    got = arrive(far, 0, shard, (partials[0],))
    own = own_sum(got, order, hiddens, block)
    results, ahead = (), []
    for p, codes in enumerate(coded):
        early = p * block < part
        results = adam(
            own,
            codes,
            master_weight,
            moment_one,
            moment_two,
            p * block,
            block,
            early,
            tuple(results),
        )
        if early:
            *results, piece = results
            ahead.append(piece[0])
    new_master, new_one, new_two, peak = results

    beside = [swap(piece, 1) for piece in ahead]
    step = half
    while step:
        peak = jnp.maximum(peak, swap(peak, step))
        step //= 2
    late = scale(new_master, peak, part, part, beside)
    factor = 1.0 / (peak + peak_eps)

    def spread(piece, next_to=None):
        held, distance = [(piece, me)], half
        while distance:
            for x, source in list(held):
                if next_to is not None and distance == 1 and x is piece:
                    got = next_to
                else:
                    got = swap(x, distance)
                held.append((got, source ^ distance))
            distance //= 2
        return held

    last = spread(late)
    flows = [(part, last)]
    for p, piece in enumerate(ahead):
        flows.append((p * block, spread(gate(piece, (last[1][0],)), beside[p])))
    last[0] = (gate(late, (flows[1][1][1][0],)), me)
    whole_shape = (replicas * shard, ffn)
    scaled = None
    for i in range(replicas):
        for at, held in flows:
            got, source = held[i]
            rows = part if at == part else block
            spot = (source * shard + at) // rows
            scaled = place(scaled, whole_shape, got, spot, factor)
    return new_master, new_one, new_two, scaled, peak


def solution(mesh):
    experts, replicas = mesh.devices.shape
    cut = jax.sharding.Mesh(
        mesh.devices.reshape(experts, 2, replicas // 2), ("expert", "far", "near")
    )
    everything = ("expert", "far", "near")
    placed = P(everything, None)
    return jax.shard_map(
        local,
        mesh=cut,
        in_specs=(placed, placed, P(everything), placed, placed, placed),
        out_specs=(placed, placed, placed, P("expert", None), P("expert")),
        check_vma=False,
    )
```

```python
import functools
import jax
import jax.numpy as jnp
from jax import lax
from jax.experimental import pallas as pl
from jax.experimental.pallas import tpu as pltpu
from jax.sharding import PartitionSpec as P

beta_one = 0.9
beta_two = 0.999
correct_one = 1.0 - 0.9**5
correct_two = 1.0 - 0.999**5
adam_eps = 1e-08
learn_rate = 0.05
weight_decay = 1.0
peak_eps = 1e-06

MIB = 1024 * 1024
LEVELS = 32000.0
PLACE_HINT = 1 << 30
TAIL = 16


def params(mib=24):
    return pltpu.CompilerParams(vmem_limit_bytes=mib * MIB)


def hint(amount):
    return pl.CostEstimate(flops=amount, bytes_accessed=amount, transcendentals=0)


def pick_kernel(strips, table_ref, x_ref, out_ref, buffer, sems_in, sems_out):
    rows = x_ref.shape[0]
    width = out_ref.shape[1]
    size = rows // strips
    moves = []
    for k in range(out_ref.shape[0] // size):
        i, j = divmod(k, strips)
        start = pl.multiple_of(table_ref[i] * width, width)
        there = pl.ds(k * size, size)
        moves.append(
            (
                pltpu.make_async_copy(
                    x_ref.at[pl.ds(j * size, size), pl.ds(start, width)],
                    buffer.at[there, :],
                    sems_in.at[k],
                ),
                pltpu.make_async_copy(buffer.at[there, :], out_ref.at[there, :], sems_out.at[k]),
            )
        )
    for come, _ in moves:
        come.start()
    for come, go in moves:
        come.wait()
        go.start()
    for _, go in moves:
        go.wait()


def pick_columns(x, chunks, width):
    rows, count, strips = x.shape[0], chunks.shape[0], 4
    anywhere = pl.BlockSpec(memory_space=pl.ANY)
    return pl.pallas_call(
        functools.partial(pick_kernel, strips),
        out_shape=jax.ShapeDtypeStruct((count * rows, width), x.dtype),
        in_specs=[pl.BlockSpec(memory_space=pltpu.SMEM), anywhere],
        out_specs=anywhere,
        scratch_shapes=[
            pltpu.VMEM((count * rows, width), x.dtype),
            pltpu.SemaphoreType.DMA((strips * count,)),
            pltpu.SemaphoreType.DMA((strips * count,)),
        ],
        compiler_params=params(60),
        cost_estimate=hint(1024),
        name="pick_columns",
    )(chunks, x)


def gate_kernel(*refs):
    pass


def gate(x, after, work=1024):
    if not after and work == 1024:
        return x
    anywhere = pl.BlockSpec(memory_space=pl.ANY)
    return pl.pallas_call(
        gate_kernel,
        out_shape=jax.ShapeDtypeStruct(x.shape, x.dtype),
        in_specs=[anywhere] * (1 + len(after)),
        out_specs=anywhere,
        input_output_aliases={0: 0},
        cost_estimate=hint(work),
        name="gate",
    )(x, *after)


def contract(rows_ref, hidden_ref):
    return lax.dot_general(
        rows_ref[...],
        hidden_ref[...],
        (((0,), (0,)), ((), ())),
        preferred_element_type=jnp.float32,
    )


def group_sum(count, refs):
    rows, hidden = refs[1 : count + 1], refs[count + 1 : 2 * count + 1]
    total = contract(rows[0], hidden[0])
    for k in range(1, count):
        total = total + contract(rows[k], hidden[k])
    return total


def encode(values, out):
    block = values.shape[0]
    top = jnp.maximum(jnp.max(jnp.abs(values), axis=0, keepdims=True), 1e-30)
    exponent = jnp.floor(jnp.log2(top)) + 1.0
    codes = jnp.round(values * (1.0 / (jnp.exp2(exponent) * (1.0 / LEVELS))))
    out[:block, :] = codes.astype(jnp.int32).astype(jnp.int16)
    out[block:, :] = jnp.broadcast_to(
        exponent.astype(jnp.int32), (TAIL, values.shape[1])
    ).astype(jnp.int16)


def decode(coded, rows):
    block = coded.shape[0] - TAIL
    exponent = coded[block : block + 1, :].astype(jnp.int32).astype(jnp.float32)
    codes = coded[rows, :].astype(jnp.int32).astype(jnp.float32)
    return codes * (jnp.exp2(exponent) * (1.0 / LEVELS))


def code_kernel(count, *refs):
    encode(group_sum(count, refs), refs[-1].at[0])


def sum_kernel(count, *refs):
    refs[-1][...] = group_sum(count, refs)


def summed(kernel, rows, order, hidden, at, width, block, out_shape, out_spec, name):
    count = len(hidden)
    depth, ffn = hidden[0].shape
    first = at // block
    return pl.pallas_call(
        functools.partial(kernel, count),
        out_shape=out_shape,
        grid_spec=pltpu.PrefetchScalarGridSpec(
            num_scalar_prefetch=1,
            grid=(width // block,),
            in_specs=[
                pl.BlockSpec(
                    (depth, block), functools.partial(lambda k, i, table: (table[k], first + i), k)
                )
                for k in range(count)
            ]
            + [pl.BlockSpec((depth, ffn), lambda i, table: (0, 0))] * count,
            out_specs=out_spec,
        ),
        compiler_params=params(),
        cost_estimate=hint(1024),
        name=name,
    )(order, *[rows] * count, *hidden)


def coded_sum(rows, order, hidden, at, width, block):
    ffn = hidden[0].shape[1]
    shape = jax.ShapeDtypeStruct((width // block, block + TAIL, ffn), jnp.int16)
    spec = pl.BlockSpec((1, block + TAIL, ffn), lambda i, table: (i, 0, 0))
    return summed(
        code_kernel, rows, order, hidden, at, width, block, shape, spec, "coded_sum"
    )


def own_sum(rows, order, hidden, block):
    ffn, width = hidden[0].shape[1], rows.shape[1]
    shape = jax.ShapeDtypeStruct((width, ffn), jnp.float32)
    spec = pl.BlockSpec((block, ffn), lambda i, table: (i, 0))
    return summed(sum_kernel, rows, order, hidden, 0, width, block, shape, spec, "own_sum")


def adam_kernel(arrays, at, block, size, ahead, *refs):
    streams = refs[:5]
    refs, (early,) = (refs[:-11] + refs[-10:], refs[-11:-10]) if ahead else (refs, (None,))
    outs, top_ref = refs[-14:-11], refs[-11]
    buffers, results = refs[-10:-5], refs[-5:-2]
    arrived, left = refs[-2:]
    own, coded, master, one, two = buffers
    steps = coded.shape[0] * block // size
    comes, leaves = [], []
    for i in range(steps):
        here, there = pl.ds(i * size, size), pl.ds(at + i * size, size)
        pairs = [(x.at[there, :], y.at[here, :]) for x, y in zip(streams[2:], buffers[2:])]
        pairs.append((streams[0].at[there, :], own.at[here, :]))
        if i * size % block == 0:
            b = i * size // block
            pairs.append((streams[1].at[b], coded.at[b]))
        comes.append(
            [pltpu.make_async_copy(x, y, arrived.at[i, k]) for k, (x, y) in enumerate(pairs)]
        )
        leaves.append(
            [
                pltpu.make_async_copy(y.at[here, :], x.at[there, :], left.at[i, k])
                for k, (x, y) in enumerate(zip(outs, results))
            ]
        )
    for copies in comes:
        for copy in copies:
            copy.start()
    highest = None
    for i in range(steps):
        for copy in comes[i]:
            copy.wait()
        here = pl.ds(i * size, size)
        b, off = i * size // block, i * size % block
        grad = own[here, :] + decode(coded.at[b], pl.ds(off, size))
        first = beta_one * one[here, :].astype(jnp.float32) + (1.0 - beta_one) * grad
        second = beta_two * two[here, :].astype(jnp.float32) + (1.0 - beta_two) * grad * grad
        update = (first * (1.0 / correct_one)) / (
            jnp.sqrt(second * (1.0 / correct_two)) + adam_eps
        )
        weight = master[here, :]
        new_master = weight - learn_rate * (update + weight_decay * weight)
        results[0][here, :] = new_master
        results[1][here, :] = first.astype(jnp.bfloat16)
        results[2][here, :] = second.astype(jnp.bfloat16)
        for copy in leaves[i]:
            copy.start()
        top = jnp.max(jnp.abs(new_master), axis=0, keepdims=True)
        highest = top if highest is None else jnp.maximum(highest, top)
        if ahead and off + size == block:
            encode(results[0][pl.ds(b * block, block), :], early.at[b])
    peak = jnp.max(highest)
    if arrays:
        peak = jnp.maximum(peak, refs[5 + arrays][0])
    top_ref[0] = peak
    for copies in leaves:
        for copy in copies:
            copy.wait()


def adam(own, coded, master, one, two, at, block, ahead, earlier=()):
    shard, ffn = master.shape
    size = min(128, block)
    width = coded.shape[0] * block
    steps = width // size
    anywhere = pl.BlockSpec(memory_space=pl.ANY)
    scalar = pl.BlockSpec(memory_space=pltpu.SMEM)
    arrays = max(len(earlier) - 1, 0)
    types = (jnp.float32, jnp.bfloat16, jnp.bfloat16)
    return pl.pallas_call(
        functools.partial(adam_kernel, arrays, at, block, size, ahead),
        out_shape=tuple(jax.ShapeDtypeStruct((shard, ffn), t) for t in types)
        + (jax.ShapeDtypeStruct((1,), jnp.float32),)
        + (jax.ShapeDtypeStruct(coded.shape, jnp.int16),) * ahead,
        in_specs=[anywhere] * (5 + arrays) + [scalar] * (arrays > 0),
        out_specs=(anywhere, anywhere, anywhere, scalar)
        + (pl.BlockSpec(memory_space=pltpu.VMEM),) * ahead,
        scratch_shapes=[pltpu.VMEM((width, ffn), jnp.float32), pltpu.VMEM(coded.shape, jnp.int16)]
        + [pltpu.VMEM((width, ffn), t) for t in types * 2]
        + [pltpu.SemaphoreType.DMA((steps, 5)), pltpu.SemaphoreType.DMA((steps, 3))],
        input_output_aliases={5 + k: k for k in range(arrays)},
        compiler_params=params(60),
        cost_estimate=hint(1024),
        name="adam",
    )(own, coded, master, one, two, *earlier)


def scale_kernel(peak_ref, weight_ref, *refs):
    out_ref = refs[-1]
    factor = 1.0 / (jnp.full((1, out_ref.shape[1]), peak_ref[0], jnp.float32) + peak_eps)
    out_ref[...] = (weight_ref[...] * factor).astype(jnp.bfloat16)


def scale(weight, peak, at, rows, after):
    ffn = weight.shape[1]
    block = rows // 2
    return pl.pallas_call(
        scale_kernel,
        out_shape=jax.ShapeDtypeStruct((rows, ffn), jnp.bfloat16),
        grid=(2,),
        in_specs=[
            pl.BlockSpec(memory_space=pltpu.SMEM),
            pl.BlockSpec((block, ffn), lambda i: (at // block + i, 0)),
        ]
        + [pl.BlockSpec(memory_space=pl.ANY)] * len(after),
        out_specs=pl.BlockSpec((block, ffn), lambda i: (i, 0)),
        compiler_params=params(),
        cost_estimate=hint(1024),
        name="scale",
    )(peak, weight, *after)


def place_kernel(strips, coded, table_ref, factor_ref, piece, *refs):
    whole, landed, scaled, sems_in, sems_out = refs[-5:]
    rows = scaled.shape[0]
    size = rows // strips
    at = pl.multiple_of(table_ref[0] * rows, rows)
    comes, leaves = [], []
    for j in range(strips):
        here = pl.ds(j * size, size)
        comes.append(
            pltpu.make_async_copy(piece.at[here, :], landed.at[here, :], sems_in.at[j])
        )
        leaves.append(
            pltpu.make_async_copy(
                (scaled if coded else landed).at[here, :],
                whole.at[pl.ds(at + j * size, size), :],
                sems_out.at[j],
            )
        )
    if coded:
        last = pl.ds(rows, TAIL)
        comes.append(
            pltpu.make_async_copy(piece.at[last, :], landed.at[last, :], sems_in.at[strips])
        )
    for copy in comes:
        copy.start()
    if coded:
        comes[-1].wait()
    for j in range(strips):
        comes[j].wait()
        if coded:
            here = pl.ds(j * size, size)
            values = decode(landed, here) * factor_ref[0]
            scaled[here, :] = values.astype(jnp.bfloat16)
        leaves[j].start()
    for copy in leaves:
        copy.wait()


def place(whole, shape, piece, spot, factor):
    coded = piece.dtype == jnp.int16
    rows, ffn = piece.shape
    rows -= TAIL * coded
    strips = 4
    anywhere = pl.BlockSpec(memory_space=pl.ANY)
    scalars = pl.BlockSpec(memory_space=pltpu.SMEM)
    earlier = () if whole is None else (whole,)
    return pl.pallas_call(
        functools.partial(place_kernel, strips, coded),
        out_shape=jax.ShapeDtypeStruct(shape, jnp.bfloat16),
        in_specs=[scalars, scalars, anywhere] + [anywhere] * len(earlier),
        out_specs=anywhere,
        scratch_shapes=[
            pltpu.VMEM(piece.shape, piece.dtype),
            pltpu.VMEM((rows, ffn), jnp.bfloat16),
            pltpu.SemaphoreType.DMA((strips + 1,)),
            pltpu.SemaphoreType.DMA((strips,)),
        ],
        input_output_aliases={3: 0} if earlier else {},
        compiler_params=params(),
        cost_estimate=hint(PLACE_HINT),
        name="place",
    )(spot.astype(jnp.int32).reshape(1), factor, piece, *earlier)


def local(out_grad, hidden_saved, recv_counts, master_weight, moment_one, moment_two):
    experts = lax.axis_size("expert")
    half = lax.axis_size("near")
    replicas = lax.axis_size("far") * half
    near, far = lax.axis_index("near"), lax.axis_index("far")
    me = far * half + near
    capacity = out_grad.shape[0] // experts
    shard, ffn = master_weight.shape
    block, part = min(256, shard // 2), shard // 2
    chain = ("far", "near")

    def swap(x, k):
        return lax.ppermute(x, chain, [(i, i ^ k) for i in range(replicas)])

    live = (jnp.arange(capacity)[None, :] < recv_counts[:, None]).reshape(-1)
    hidden = jnp.where(live[:, None], hidden_saved, jnp.zeros((), jnp.bfloat16))
    hiddens = [hidden] + [gate(swap(hidden, k), (), 1 << 35) for k in range(1, half)]
    order = jnp.stack([near ^ k for k in range(half)]).astype(jnp.int32)

    def arrive(side, at, width, after):
        chunks = ((side * half + jnp.arange(half)) * shard + at) // width
        picked = gate(pick_columns(out_grad, chunks.astype(jnp.int32), width), after)
        return lax.all_to_all(picked, ("near", "expert"), 0, 0, tiled=True)

    got = arrive(1 - far, 0, shard, ())
    partials = [
        coded_sum(got, order, hiddens, at, block, block) for at in range(0, shard, block)
    ]
    coded = [swap(partial, half) for partial in partials]
    coded[0] = gate(coded[0], (), 1 << 35)

    got = arrive(far, 0, shard, (partials[0],))
    own = own_sum(got, order, hiddens, block)
    results, ahead = (), []
    for p, codes in enumerate(coded):
        early = p * block < part
        results = adam(
            own,
            codes,
            master_weight,
            moment_one,
            moment_two,
            p * block,
            block,
            early,
            tuple(results),
        )
        if early:
            *results, piece = results
            ahead.append(piece[0])
    new_master, new_one, new_two, peak = results

    beside = [swap(piece, 1) for piece in ahead]
    step = half
    while step:
        peak = jnp.maximum(peak, swap(peak, step))
        step //= 2
    late = scale(new_master, peak, part, part, beside)
    factor = 1.0 / (peak + peak_eps)

    def spread(piece, next_to=None):
        held, distance = [(piece, me)], half
        while distance:
            for x, source in list(held):
                if next_to is not None and distance == 1 and x is piece:
                    got = next_to
                else:
                    got = swap(x, distance)
                held.append((got, source ^ distance))
            distance //= 2
        return held

    last = spread(late)
    flows = [(part, last)]
    for p, piece in enumerate(ahead):
        flows.append((p * block, spread(gate(piece, (last[1][0],)), beside[p])))
    last[0] = (gate(late, (flows[1][1][1][0],)), me)
    whole_shape = (replicas * shard, ffn)
    scaled = None
    for i in range(replicas):
        for at, held in flows:
            got, source = held[i]
            rows = part if at == part else block
            spot = (source * shard + at) // rows
            scaled = place(scaled, whole_shape, got, spot, factor)
    return new_master, new_one, new_two, scaled, peak


def solution(mesh):
    experts, replicas = mesh.devices.shape
    cut = jax.sharding.Mesh(
        mesh.devices.reshape(experts, 2, replicas // 2), ("expert", "far", "near")
    )
    everything = ("expert", "far", "near")
    placed = P(everything, None)
    return jax.shard_map(
        local,
        mesh=cut,
        in_specs=(placed, placed, P(everything), placed, placed, placed),
        out_specs=(placed, placed, placed, P("expert", None), P("expert")),
        check_vma=False,
    )
```

```python
import functools
import jax
import jax.numpy as jnp
from jax import lax
from jax.experimental import pallas as pl
from jax.experimental.pallas import tpu as pltpu
from jax.sharding import PartitionSpec as P

beta_one = 0.9
beta_two = 0.999
correct_one = 1.0 - 0.9**5
correct_two = 1.0 - 0.999**5
adam_eps = 1e-08
learn_rate = 0.05
weight_decay = 1.0
peak_eps = 1e-06

MIB = 1024 * 1024
LEVELS = 32000.0
PLACE_HINT = 1 << 30
TAIL = 16


def params(mib=24):
    return pltpu.CompilerParams(vmem_limit_bytes=mib * MIB)


def hint(amount):
    return pl.CostEstimate(flops=amount, bytes_accessed=amount, transcendentals=0)


def pick_kernel(strips, table_ref, x_ref, out_ref, buffer, sems_in, sems_out):
    rows = x_ref.shape[0]
    width = out_ref.shape[1]
    size = rows // strips
    moves = []
    for k in range(out_ref.shape[0] // size):
        i, j = divmod(k, strips)
        start = pl.multiple_of(table_ref[i] * width, width)
        there = pl.ds(k * size, size)
        moves.append(
            (
                pltpu.make_async_copy(
                    x_ref.at[pl.ds(j * size, size), pl.ds(start, width)],
                    buffer.at[there, :],
                    sems_in.at[k],
                ),
                pltpu.make_async_copy(buffer.at[there, :], out_ref.at[there, :], sems_out.at[k]),
            )
        )
    for come, _ in moves:
        come.start()
    for come, go in moves:
        come.wait()
        go.start()
    for _, go in moves:
        go.wait()


def pick_columns(x, chunks, width):
    rows, count, strips = x.shape[0], chunks.shape[0], 4
    anywhere = pl.BlockSpec(memory_space=pl.ANY)
    return pl.pallas_call(
        functools.partial(pick_kernel, strips),
        out_shape=jax.ShapeDtypeStruct((count * rows, width), x.dtype),
        in_specs=[pl.BlockSpec(memory_space=pltpu.SMEM), anywhere],
        out_specs=anywhere,
        scratch_shapes=[
            pltpu.VMEM((count * rows, width), x.dtype),
            pltpu.SemaphoreType.DMA((strips * count,)),
            pltpu.SemaphoreType.DMA((strips * count,)),
        ],
        compiler_params=params(60),
        cost_estimate=hint(1024),
        name="pick_columns",
    )(chunks, x)


def gate_kernel(*refs):
    pass


def gate(x, after, work=1024):
    if not after and work == 1024:
        return x
    anywhere = pl.BlockSpec(memory_space=pl.ANY)
    return pl.pallas_call(
        gate_kernel,
        out_shape=jax.ShapeDtypeStruct(x.shape, x.dtype),
        in_specs=[anywhere] * (1 + len(after)),
        out_specs=anywhere,
        input_output_aliases={0: 0},
        cost_estimate=hint(work),
        name="gate",
    )(x, *after)


def contract(rows_ref, hidden_ref):
    return lax.dot_general(
        rows_ref[...],
        hidden_ref[...],
        (((0,), (0,)), ((), ())),
        preferred_element_type=jnp.float32,
    )


def group_sum(count, refs):
    rows, hidden = refs[1 : count + 1], refs[count + 1 : 2 * count + 1]
    total = contract(rows[0], hidden[0])
    for k in range(1, count):
        total = total + contract(rows[k], hidden[k])
    return total


def encode(values, out):
    block = values.shape[0]
    top = jnp.maximum(jnp.max(jnp.abs(values), axis=0, keepdims=True), 1e-30)
    exponent = jnp.floor(jnp.log2(top)) + 1.0
    codes = jnp.round(values * (1.0 / (jnp.exp2(exponent) * (1.0 / LEVELS))))
    out[:block, :] = codes.astype(jnp.int32).astype(jnp.int16)
    out[block:, :] = jnp.broadcast_to(
        exponent.astype(jnp.int32), (TAIL, values.shape[1])
    ).astype(jnp.int16)


def decode(coded, rows):
    block = coded.shape[0] - TAIL
    exponent = coded[block : block + 1, :].astype(jnp.int32).astype(jnp.float32)
    codes = coded[rows, :].astype(jnp.int32).astype(jnp.float32)
    return codes * (jnp.exp2(exponent) * (1.0 / LEVELS))


def code_kernel(count, *refs):
    encode(group_sum(count, refs), refs[-1].at[0])


def sum_kernel(count, *refs):
    refs[-1][...] = group_sum(count, refs)


def summed(kernel, rows, order, hidden, at, width, block, out_shape, out_spec, name):
    count = len(hidden)
    depth, ffn = hidden[0].shape
    first = at // block
    return pl.pallas_call(
        functools.partial(kernel, count),
        out_shape=out_shape,
        grid_spec=pltpu.PrefetchScalarGridSpec(
            num_scalar_prefetch=1,
            grid=(width // block,),
            in_specs=[
                pl.BlockSpec(
                    (depth, block), functools.partial(lambda k, i, table: (table[k], first + i), k)
                )
                for k in range(count)
            ]
            + [pl.BlockSpec((depth, ffn), lambda i, table: (0, 0))] * count,
            out_specs=out_spec,
        ),
        compiler_params=params(),
        cost_estimate=hint(1024),
        name=name,
    )(order, *[rows] * count, *hidden)


def coded_sum(rows, order, hidden, at, width, block):
    ffn = hidden[0].shape[1]
    shape = jax.ShapeDtypeStruct((width // block, block + TAIL, ffn), jnp.int16)
    spec = pl.BlockSpec((1, block + TAIL, ffn), lambda i, table: (i, 0, 0))
    return summed(
        code_kernel, rows, order, hidden, at, width, block, shape, spec, "coded_sum"
    )


def own_sum(rows, order, hidden, block):
    ffn, width = hidden[0].shape[1], rows.shape[1]
    shape = jax.ShapeDtypeStruct((width, ffn), jnp.float32)
    spec = pl.BlockSpec((block, ffn), lambda i, table: (i, 0))
    return summed(sum_kernel, rows, order, hidden, 0, width, block, shape, spec, "own_sum")


def adam_kernel(arrays, at, block, size, ahead, *refs):
    streams = refs[:5]
    refs, (early,) = (refs[:-11] + refs[-10:], refs[-11:-10]) if ahead else (refs, (None,))
    outs, top_ref = refs[-14:-11], refs[-11]
    buffers, results = refs[-10:-5], refs[-5:-2]
    arrived, left = refs[-2:]
    own, coded, master, one, two = buffers
    steps = coded.shape[0] * block // size
    comes, leaves = [], []
    for i in range(steps):
        here, there = pl.ds(i * size, size), pl.ds(at + i * size, size)
        pairs = [(x.at[there, :], y.at[here, :]) for x, y in zip(streams[2:], buffers[2:])]
        pairs.append((streams[0].at[there, :], own.at[here, :]))
        if i * size % block == 0:
            b = i * size // block
            pairs.append((streams[1].at[b], coded.at[b]))
        comes.append(
            [pltpu.make_async_copy(x, y, arrived.at[i, k]) for k, (x, y) in enumerate(pairs)]
        )
        leaves.append(
            [
                pltpu.make_async_copy(y.at[here, :], x.at[there, :], left.at[i, k])
                for k, (x, y) in enumerate(zip(outs, results))
            ]
        )
    for copies in comes:
        for copy in copies:
            copy.start()
    highest = None
    for i in range(steps):
        for copy in comes[i]:
            copy.wait()
        here = pl.ds(i * size, size)
        b, off = i * size // block, i * size % block
        grad = own[here, :] + decode(coded.at[b], pl.ds(off, size))
        first = beta_one * one[here, :].astype(jnp.float32) + (1.0 - beta_one) * grad
        second = beta_two * two[here, :].astype(jnp.float32) + (1.0 - beta_two) * grad * grad
        update = (first * (1.0 / correct_one)) / (
            jnp.sqrt(second * (1.0 / correct_two)) + adam_eps
        )
        weight = master[here, :]
        new_master = weight - learn_rate * (update + weight_decay * weight)
        results[0][here, :] = new_master
        results[1][here, :] = first.astype(jnp.bfloat16)
        results[2][here, :] = second.astype(jnp.bfloat16)
        for copy in leaves[i]:
            copy.start()
        top = jnp.max(jnp.abs(new_master), axis=0, keepdims=True)
        highest = top if highest is None else jnp.maximum(highest, top)
        if ahead and off + size == block:
            encode(results[0][pl.ds(b * block, block), :], early.at[b])
    peak = jnp.max(highest)
    if arrays:
        peak = jnp.maximum(peak, refs[5 + arrays][0])
    top_ref[0] = peak
    for copies in leaves:
        for copy in copies:
            copy.wait()


def adam(own, coded, master, one, two, at, block, ahead, earlier=()):
    shard, ffn = master.shape
    size = min(128, block)
    width = coded.shape[0] * block
    steps = width // size
    anywhere = pl.BlockSpec(memory_space=pl.ANY)
    scalar = pl.BlockSpec(memory_space=pltpu.SMEM)
    arrays = max(len(earlier) - 1, 0)
    types = (jnp.float32, jnp.bfloat16, jnp.bfloat16)
    return pl.pallas_call(
        functools.partial(adam_kernel, arrays, at, block, size, ahead),
        out_shape=tuple(jax.ShapeDtypeStruct((shard, ffn), t) for t in types)
        + (jax.ShapeDtypeStruct((1,), jnp.float32),)
        + (jax.ShapeDtypeStruct(coded.shape, jnp.int16),) * ahead,
        in_specs=[anywhere] * (5 + arrays) + [scalar] * (arrays > 0),
        out_specs=(anywhere, anywhere, anywhere, scalar)
        + (pl.BlockSpec(memory_space=pltpu.VMEM),) * ahead,
        scratch_shapes=[pltpu.VMEM((width, ffn), jnp.float32), pltpu.VMEM(coded.shape, jnp.int16)]
        + [pltpu.VMEM((width, ffn), t) for t in types * 2]
        + [pltpu.SemaphoreType.DMA((steps, 5)), pltpu.SemaphoreType.DMA((steps, 3))],
        input_output_aliases={5 + k: k for k in range(arrays)},
        compiler_params=params(60),
        cost_estimate=hint(1024),
        name="adam",
    )(own, coded, master, one, two, *earlier)


def scale_kernel(peak_ref, weight_ref, *refs):
    out_ref = refs[-1]
    factor = 1.0 / (jnp.full((1, out_ref.shape[1]), peak_ref[0], jnp.float32) + peak_eps)
    out_ref[...] = (weight_ref[...] * factor).astype(jnp.bfloat16)


def scale(weight, peak, at, rows, after):
    ffn = weight.shape[1]
    block = rows // 2
    return pl.pallas_call(
        scale_kernel,
        out_shape=jax.ShapeDtypeStruct((rows, ffn), jnp.bfloat16),
        grid=(2,),
        in_specs=[
            pl.BlockSpec(memory_space=pltpu.SMEM),
            pl.BlockSpec((block, ffn), lambda i: (at // block + i, 0)),
        ]
        + [pl.BlockSpec(memory_space=pl.ANY)] * len(after),
        out_specs=pl.BlockSpec((block, ffn), lambda i: (i, 0)),
        compiler_params=params(),
        cost_estimate=hint(1024),
        name="scale",
    )(peak, weight, *after)


def place_kernel(strips, coded, table_ref, factor_ref, piece, *refs):
    whole, landed, scaled, sems_in, sems_out = refs[-5:]
    rows = scaled.shape[0]
    size = rows // strips
    at = pl.multiple_of(table_ref[0] * rows, rows)
    comes, leaves = [], []
    for j in range(strips):
        here = pl.ds(j * size, size)
        comes.append(
            pltpu.make_async_copy(piece.at[here, :], landed.at[here, :], sems_in.at[j])
        )
        leaves.append(
            pltpu.make_async_copy(
                (scaled if coded else landed).at[here, :],
                whole.at[pl.ds(at + j * size, size), :],
                sems_out.at[j],
            )
        )
    if coded:
        last = pl.ds(rows, TAIL)
        comes.append(
            pltpu.make_async_copy(piece.at[last, :], landed.at[last, :], sems_in.at[strips])
        )
    for copy in comes:
        copy.start()
    if coded:
        comes[-1].wait()
    for j in range(strips):
        comes[j].wait()
        if coded:
            here = pl.ds(j * size, size)
            values = decode(landed, here) * factor_ref[0]
            scaled[here, :] = values.astype(jnp.bfloat16)
        leaves[j].start()
    for copy in leaves:
        copy.wait()


def place(whole, shape, piece, spot, factor):
    coded = piece.dtype == jnp.int16
    rows, ffn = piece.shape
    rows -= TAIL * coded
    strips = 4
    anywhere = pl.BlockSpec(memory_space=pl.ANY)
    scalars = pl.BlockSpec(memory_space=pltpu.SMEM)
    earlier = () if whole is None else (whole,)
    return pl.pallas_call(
        functools.partial(place_kernel, strips, coded),
        out_shape=jax.ShapeDtypeStruct(shape, jnp.bfloat16),
        in_specs=[scalars, scalars, anywhere] + [anywhere] * len(earlier),
        out_specs=anywhere,
        scratch_shapes=[
            pltpu.VMEM(piece.shape, piece.dtype),
            pltpu.VMEM((rows, ffn), jnp.bfloat16),
            pltpu.SemaphoreType.DMA((strips + 1,)),
            pltpu.SemaphoreType.DMA((strips,)),
        ],
        input_output_aliases={3: 0} if earlier else {},
        compiler_params=params(),
        cost_estimate=hint(PLACE_HINT),
        name="place",
    )(spot.astype(jnp.int32).reshape(1), factor, piece, *earlier)


def local(out_grad, hidden_saved, recv_counts, master_weight, moment_one, moment_two):
    experts = lax.axis_size("expert")
    half = lax.axis_size("near")
    replicas = lax.axis_size("far") * half
    near, far = lax.axis_index("near"), lax.axis_index("far")
    me = far * half + near
    capacity = out_grad.shape[0] // experts
    shard, ffn = master_weight.shape
    block, part = min(256, shard // 2), shard // 2
    chain = ("far", "near")

    def swap(x, k):
        return lax.ppermute(x, chain, [(i, i ^ k) for i in range(replicas)])

    live = (jnp.arange(capacity)[None, :] < recv_counts[:, None]).reshape(-1)
    hidden = jnp.where(live[:, None], hidden_saved, jnp.zeros((), jnp.bfloat16))
    hiddens = [hidden] + [gate(swap(hidden, k), (), 1 << 35) for k in range(1, half)]
    order = jnp.stack([near ^ k for k in range(half)]).astype(jnp.int32)

    def arrive(side, at, width, after):
        chunks = ((side * half + jnp.arange(half)) * shard + at) // width
        picked = gate(pick_columns(out_grad, chunks.astype(jnp.int32), width), after)
        return lax.all_to_all(picked, ("near", "expert"), 0, 0, tiled=True)

    got = arrive(1 - far, 0, shard, ())
    partials = [
        coded_sum(got, order, hiddens, at, block, block) for at in range(0, shard, block)
    ]
    coded = [swap(partial, half) for partial in partials]
    coded[0] = gate(coded[0], (), 1 << 35)

    got = arrive(far, 0, shard, (partials[0],))
    own = own_sum(got, order, hiddens, block)
    results, ahead = (), []
    for p, codes in enumerate(coded):
        early = p * block < part
        results = adam(
            own,
            codes,
            master_weight,
            moment_one,
            moment_two,
            p * block,
            block,
            early,
            tuple(results),
        )
        if early:
            *results, piece = results
            ahead.append(piece[0])
    new_master, new_one, new_two, peak = results

    beside = [gate(swap(piece, 1), (), work) for piece, work in zip(ahead, (1<<34, 1024))]
    step = half
    while step:
        peak = jnp.maximum(peak, swap(peak, step))
        step //= 2
    late = scale(new_master, peak, part, part, beside)
    factor = 1.0 / (peak + peak_eps)

    def spread(piece, next_to=None):
        held, distance = [(piece, me)], half
        while distance:
            for x, source in list(held):
                if next_to is not None and distance == 1 and x is piece:
                    got = next_to
                else:
                    got = swap(x, distance)
                held.append((got, source ^ distance))
            distance //= 2
        return held

    last = spread(late)
    flows = [(part, last)]
    for p, piece in enumerate(ahead):
        flows.append((p * block, spread(gate(piece, (last[1][0],)), beside[p])))
    last[0] = (gate(late, (flows[1][1][1][0],)), me)
    whole_shape = (replicas * shard, ffn)
    scaled = None
    for i in range(replicas):
        for at, held in flows:
            got, source = held[i]
            rows = part if at == part else block
            spot = (source * shard + at) // rows
            scaled = place(scaled, whole_shape, got, spot, factor)
    return new_master, new_one, new_two, scaled, peak


def solution(mesh):
    experts, replicas = mesh.devices.shape
    cut = jax.sharding.Mesh(
        mesh.devices.reshape(experts, 2, replicas // 2), ("expert", "far", "near")
    )
    everything = ("expert", "far", "near")
    placed = P(everything, None)
    return jax.shard_map(
        local,
        mesh=cut,
        in_specs=(placed, placed, P(everything), placed, placed, placed),
        out_specs=(placed, placed, placed, P("expert", None), P("expert")),
        check_vma=False,
    )
```

```python
import functools
import jax
import jax.numpy as jnp
from jax import lax
from jax.experimental import pallas as pl
from jax.experimental.pallas import tpu as pltpu
from jax.sharding import PartitionSpec as P

beta_one = 0.9
beta_two = 0.999
correct_one = 1.0 - 0.9**5
correct_two = 1.0 - 0.999**5
adam_eps = 1e-08
learn_rate = 0.05
weight_decay = 1.0
peak_eps = 1e-06

MIB = 1024 * 1024
LEVELS = 32000.0
PLACE_HINT = 1 << 30
TAIL = 16


def params(mib=24):
    return pltpu.CompilerParams(vmem_limit_bytes=mib * MIB)


def hint(amount):
    return pl.CostEstimate(flops=amount, bytes_accessed=amount, transcendentals=0)


def pick_kernel(strips, table_ref, x_ref, out_ref, buffer, sems_in, sems_out):
    rows = x_ref.shape[0]
    width = out_ref.shape[1]
    size = rows // strips
    moves = []
    for k in range(out_ref.shape[0] // size):
        i, j = divmod(k, strips)
        start = pl.multiple_of(table_ref[i] * width, width)
        there = pl.ds(k * size, size)
        moves.append(
            (
                pltpu.make_async_copy(
                    x_ref.at[pl.ds(j * size, size), pl.ds(start, width)],
                    buffer.at[there, :],
                    sems_in.at[k],
                ),
                pltpu.make_async_copy(buffer.at[there, :], out_ref.at[there, :], sems_out.at[k]),
            )
        )
    for come, _ in moves:
        come.start()
    for come, go in moves:
        come.wait()
        go.start()
    for _, go in moves:
        go.wait()


def pick_columns(x, chunks, width):
    rows, count, strips = x.shape[0], chunks.shape[0], 4
    anywhere = pl.BlockSpec(memory_space=pl.ANY)
    return pl.pallas_call(
        functools.partial(pick_kernel, strips),
        out_shape=jax.ShapeDtypeStruct((count * rows, width), x.dtype),
        in_specs=[pl.BlockSpec(memory_space=pltpu.SMEM), anywhere],
        out_specs=anywhere,
        scratch_shapes=[
            pltpu.VMEM((count * rows, width), x.dtype),
            pltpu.SemaphoreType.DMA((strips * count,)),
            pltpu.SemaphoreType.DMA((strips * count,)),
        ],
        compiler_params=params(60),
        cost_estimate=hint(1024),
        name="pick_columns",
    )(chunks, x)


def gate_kernel(*refs):
    pass


def gate(x, after, work=1024):
    if not after and work == 1024:
        return x
    anywhere = pl.BlockSpec(memory_space=pl.ANY)
    return pl.pallas_call(
        gate_kernel,
        out_shape=jax.ShapeDtypeStruct(x.shape, x.dtype),
        in_specs=[anywhere] * (1 + len(after)),
        out_specs=anywhere,
        input_output_aliases={0: 0},
        cost_estimate=hint(work),
        name="gate",
    )(x, *after)


def contract(rows_ref, hidden_ref):
    return lax.dot_general(
        rows_ref[...],
        hidden_ref[...],
        (((0,), (0,)), ((), ())),
        preferred_element_type=jnp.float32,
    )


def group_sum(count, refs):
    rows, hidden = refs[1 : count + 1], refs[count + 1 : 2 * count + 1]
    total = contract(rows[0], hidden[0])
    for k in range(1, count):
        total = total + contract(rows[k], hidden[k])
    return total


def encode(values, out):
    block = values.shape[0]
    top = jnp.maximum(jnp.max(jnp.abs(values), axis=0, keepdims=True), 1e-30)
    exponent = jnp.floor(jnp.log2(top)) + 1.0
    codes = jnp.round(values * (1.0 / (jnp.exp2(exponent) * (1.0 / LEVELS))))
    out[:block, :] = codes.astype(jnp.int32).astype(jnp.int16)
    out[block:, :] = jnp.broadcast_to(
        exponent.astype(jnp.int32), (TAIL, values.shape[1])
    ).astype(jnp.int16)


def decode(coded, rows):
    block = coded.shape[0] - TAIL
    exponent = coded[block : block + 1, :].astype(jnp.int32).astype(jnp.float32)
    codes = coded[rows, :].astype(jnp.int32).astype(jnp.float32)
    return codes * (jnp.exp2(exponent) * (1.0 / LEVELS))


def code_kernel(count, *refs):
    encode(group_sum(count, refs), refs[-1].at[0])


def sum_kernel(count, *refs):
    refs[-1][...] = group_sum(count, refs)


def summed(kernel, rows, order, hidden, at, width, block, out_shape, out_spec, name):
    count = len(hidden)
    depth, ffn = hidden[0].shape
    first = at // block
    return pl.pallas_call(
        functools.partial(kernel, count),
        out_shape=out_shape,
        grid_spec=pltpu.PrefetchScalarGridSpec(
            num_scalar_prefetch=1,
            grid=(width // block,),
            in_specs=[
                pl.BlockSpec(
                    (depth, block), functools.partial(lambda k, i, table: (table[k], first + i), k)
                )
                for k in range(count)
            ]
            + [pl.BlockSpec((depth, ffn), lambda i, table: (0, 0))] * count,
            out_specs=out_spec,
        ),
        compiler_params=params(),
        cost_estimate=hint(1024),
        name=name,
    )(order, *[rows] * count, *hidden)


def coded_sum(rows, order, hidden, at, width, block):
    ffn = hidden[0].shape[1]
    shape = jax.ShapeDtypeStruct((width // block, block + TAIL, ffn), jnp.int16)
    spec = pl.BlockSpec((1, block + TAIL, ffn), lambda i, table: (i, 0, 0))
    return summed(
        code_kernel, rows, order, hidden, at, width, block, shape, spec, "coded_sum"
    )


def own_sum(rows, order, hidden, block):
    ffn, width = hidden[0].shape[1], rows.shape[1]
    shape = jax.ShapeDtypeStruct((width, ffn), jnp.float32)
    spec = pl.BlockSpec((block, ffn), lambda i, table: (i, 0))
    return summed(sum_kernel, rows, order, hidden, 0, width, block, shape, spec, "own_sum")


def adam_kernel(arrays, at, block, size, ahead, *refs):
    streams = refs[:5]
    refs, (early,) = (refs[:-11] + refs[-10:], refs[-11:-10]) if ahead else (refs, (None,))
    outs, top_ref = refs[-14:-11], refs[-11]
    buffers, results = refs[-10:-5], refs[-5:-2]
    arrived, left = refs[-2:]
    own, coded, master, one, two = buffers
    steps = coded.shape[0] * block // size
    comes, leaves = [], []
    for i in range(steps):
        here, there = pl.ds(i * size, size), pl.ds(at + i * size, size)
        pairs = [(x.at[there, :], y.at[here, :]) for x, y in zip(streams[2:], buffers[2:])]
        pairs.append((streams[0].at[there, :], own.at[here, :]))
        if i * size % block == 0:
            b = i * size // block
            pairs.append((streams[1].at[b], coded.at[b]))
        comes.append(
            [pltpu.make_async_copy(x, y, arrived.at[i, k]) for k, (x, y) in enumerate(pairs)]
        )
        leaves.append(
            [
                pltpu.make_async_copy(y.at[here, :], x.at[there, :], left.at[i, k])
                for k, (x, y) in enumerate(zip(outs, results))
            ]
        )
    for copies in comes:
        for copy in copies:
            copy.start()
    highest = None
    for i in range(steps):
        for copy in comes[i]:
            copy.wait()
        here = pl.ds(i * size, size)
        b, off = i * size // block, i * size % block
        grad = own[here, :] + decode(coded.at[b], pl.ds(off, size))
        first = beta_one * one[here, :].astype(jnp.float32) + (1.0 - beta_one) * grad
        second = beta_two * two[here, :].astype(jnp.float32) + (1.0 - beta_two) * grad * grad
        update = (first * (1.0 / correct_one)) / (
            jnp.sqrt(second * (1.0 / correct_two)) + adam_eps
        )
        weight = master[here, :]
        new_master = weight - learn_rate * (update + weight_decay * weight)
        results[0][here, :] = new_master
        results[1][here, :] = first.astype(jnp.bfloat16)
        results[2][here, :] = second.astype(jnp.bfloat16)
        for copy in leaves[i]:
            copy.start()
        top = jnp.max(jnp.abs(new_master), axis=0, keepdims=True)
        highest = top if highest is None else jnp.maximum(highest, top)
        if ahead and off + size == block:
            encode(results[0][pl.ds(b * block, block), :], early.at[b])
    peak = jnp.max(highest)
    if arrays:
        peak = jnp.maximum(peak, refs[5 + arrays][0])
    top_ref[0] = peak
    for copies in leaves:
        for copy in copies:
            copy.wait()


def adam(own, coded, master, one, two, at, block, ahead, earlier=()):
    shard, ffn = master.shape
    size = min(128, block)
    width = coded.shape[0] * block
    steps = width // size
    anywhere = pl.BlockSpec(memory_space=pl.ANY)
    scalar = pl.BlockSpec(memory_space=pltpu.SMEM)
    arrays = max(len(earlier) - 1, 0)
    types = (jnp.float32, jnp.bfloat16, jnp.bfloat16)
    return pl.pallas_call(
        functools.partial(adam_kernel, arrays, at, block, size, ahead),
        out_shape=tuple(jax.ShapeDtypeStruct((shard, ffn), t) for t in types)
        + (jax.ShapeDtypeStruct((1,), jnp.float32),)
        + (jax.ShapeDtypeStruct(coded.shape, jnp.int16),) * ahead,
        in_specs=[anywhere] * (5 + arrays) + [scalar] * (arrays > 0),
        out_specs=(anywhere, anywhere, anywhere, scalar)
        + (pl.BlockSpec(memory_space=pltpu.VMEM),) * ahead,
        scratch_shapes=[pltpu.VMEM((width, ffn), jnp.float32), pltpu.VMEM(coded.shape, jnp.int16)]
        + [pltpu.VMEM((width, ffn), t) for t in types * 2]
        + [pltpu.SemaphoreType.DMA((steps, 5)), pltpu.SemaphoreType.DMA((steps, 3))],
        input_output_aliases={5 + k: k for k in range(arrays)},
        compiler_params=params(60),
        cost_estimate=hint(1024),
        name="adam",
    )(own, coded, master, one, two, *earlier)


def scale_kernel(peak_ref, weight_ref, *refs):
    out_ref = refs[-1]
    factor = 1.0 / (jnp.full((1, out_ref.shape[1]), peak_ref[0], jnp.float32) + peak_eps)
    out_ref[...] = (weight_ref[...] * factor).astype(jnp.bfloat16)


def scale(weight, peak, at, rows, after):
    ffn = weight.shape[1]
    block = rows // 2
    return pl.pallas_call(
        scale_kernel,
        out_shape=jax.ShapeDtypeStruct((rows, ffn), jnp.bfloat16),
        grid=(2,),
        in_specs=[
            pl.BlockSpec(memory_space=pltpu.SMEM),
            pl.BlockSpec((block, ffn), lambda i: (at // block + i, 0)),
        ]
        + [pl.BlockSpec(memory_space=pl.ANY)] * len(after),
        out_specs=pl.BlockSpec((block, ffn), lambda i: (i, 0)),
        compiler_params=params(),
        cost_estimate=hint(1024),
        name="scale",
    )(peak, weight, *after)


def place_kernel(strips, coded, table_ref, factor_ref, piece, *refs):
    whole, landed, scaled, sems_in, sems_out = refs[-5:]
    rows = scaled.shape[0]
    size = rows // strips
    at = pl.multiple_of(table_ref[0] * rows, rows)
    comes, leaves = [], []
    for j in range(strips):
        here = pl.ds(j * size, size)
        comes.append(
            pltpu.make_async_copy(piece.at[here, :], landed.at[here, :], sems_in.at[j])
        )
        leaves.append(
            pltpu.make_async_copy(
                (scaled if coded else landed).at[here, :],
                whole.at[pl.ds(at + j * size, size), :],
                sems_out.at[j],
            )
        )
    if coded:
        last = pl.ds(rows, TAIL)
        comes.append(
            pltpu.make_async_copy(piece.at[last, :], landed.at[last, :], sems_in.at[strips])
        )
    for copy in comes:
        copy.start()
    if coded:
        comes[-1].wait()
    for j in range(strips):
        comes[j].wait()
        if coded:
            here = pl.ds(j * size, size)
            values = decode(landed, here) * factor_ref[0]
            scaled[here, :] = values.astype(jnp.bfloat16)
        leaves[j].start()
    for copy in leaves:
        copy.wait()


def place(whole, shape, piece, spot, factor):
    coded = piece.dtype == jnp.int16
    rows, ffn = piece.shape
    rows -= TAIL * coded
    strips = 4
    anywhere = pl.BlockSpec(memory_space=pl.ANY)
    scalars = pl.BlockSpec(memory_space=pltpu.SMEM)
    earlier = () if whole is None else (whole,)
    return pl.pallas_call(
        functools.partial(place_kernel, strips, coded),
        out_shape=jax.ShapeDtypeStruct(shape, jnp.bfloat16),
        in_specs=[scalars, scalars, anywhere] + [anywhere] * len(earlier),
        out_specs=anywhere,
        scratch_shapes=[
            pltpu.VMEM(piece.shape, piece.dtype),
            pltpu.VMEM((rows, ffn), jnp.bfloat16),
            pltpu.SemaphoreType.DMA((strips + 1,)),
            pltpu.SemaphoreType.DMA((strips,)),
        ],
        input_output_aliases={3: 0} if earlier else {},
        compiler_params=params(),
        cost_estimate=hint(PLACE_HINT),
        name="place",
    )(spot.astype(jnp.int32).reshape(1), factor, piece, *earlier)


def local(out_grad, hidden_saved, recv_counts, master_weight, moment_one, moment_two):
    experts = lax.axis_size("expert")
    half = lax.axis_size("near")
    replicas = lax.axis_size("far") * half
    near, far = lax.axis_index("near"), lax.axis_index("far")
    me = far * half + near
    capacity = out_grad.shape[0] // experts
    shard, ffn = master_weight.shape
    block, part = min(256, shard // 2), shard // 2
    chain = ("far", "near")

    def swap(x, k):
        return lax.ppermute(x, chain, [(i, i ^ k) for i in range(replicas)])

    live = (jnp.arange(capacity)[None, :] < recv_counts[:, None]).reshape(-1)
    hidden = jnp.where(live[:, None], hidden_saved, jnp.zeros((), jnp.bfloat16))
    hiddens = [hidden] + [gate(swap(hidden, k), (), 1 << 35) for k in range(1, half)]
    order = jnp.stack([near ^ k for k in range(half)]).astype(jnp.int32)

    def arrive(side, at, width, after):
        chunks = ((side * half + jnp.arange(half)) * shard + at) // width
        picked = gate(pick_columns(out_grad, chunks.astype(jnp.int32), width), after)
        return lax.all_to_all(picked, ("near", "expert"), 0, 0, tiled=True)

    got = arrive(1 - far, 0, shard, ())
    partials = [
        coded_sum(got, order, hiddens, at, block, block) for at in range(0, shard, block)
    ]
    coded = [swap(partial, half) for partial in partials]
    coded[0] = gate(coded[0], (), 1 << 35)

    got = arrive(far, 0, shard, (partials[0],))
    own = own_sum(got, order, hiddens, block)
    results, ahead = (), []
    for p, codes in enumerate(coded):
        early = p * block < part
        results = adam(
            own,
            codes,
            master_weight,
            moment_one,
            moment_two,
            p * block,
            block,
            early,
            tuple(results),
        )
        if early:
            *results, piece = results
            ahead.append(piece[0])
    new_master, new_one, new_two, peak = results

    beside = [gate(swap(piece, 1), (), work) for piece, work in zip(ahead, (1<<34, 1024))]
    step = 1
    while step < replicas:
        peak = jnp.maximum(peak, swap(peak, step))
        step *= 2
    late = scale(new_master, peak, part, part, beside)
    factor = 1.0 / (peak + peak_eps)

    def spread(piece, next_to=None):
        held, distance = [(piece, me)], half
        while distance:
            for x, source in list(held):
                if next_to is not None and distance == 1 and x is piece:
                    got = next_to
                else:
                    got = swap(x, distance)
                held.append((got, source ^ distance))
            distance //= 2
        return held

    last = spread(late)
    flows = [(part, last)]
    for p, piece in enumerate(ahead):
        flows.append((p * block, spread(gate(piece, (last[1][0],)), beside[p])))
    last[0] = (gate(late, (flows[1][1][1][0],)), me)
    whole_shape = (replicas * shard, ffn)
    scaled = None
    for i in range(replicas):
        for at, held in flows:
            got, source = held[i]
            rows = part if at == part else block
            spot = (source * shard + at) // rows
            scaled = place(scaled, whole_shape, got, spot, factor)
    return new_master, new_one, new_two, scaled, peak


def solution(mesh):
    experts, replicas = mesh.devices.shape
    cut = jax.sharding.Mesh(
        mesh.devices.reshape(experts, 2, replicas // 2), ("expert", "far", "near")
    )
    everything = ("expert", "far", "near")
    placed = P(everything, None)
    return jax.shard_map(
        local,
        mesh=cut,
        in_specs=(placed, placed, P(everything), placed, placed, placed),
        out_specs=(placed, placed, placed, P("expert", None), P("expert")),
        check_vma=False,
    )
```

```python
import functools
import jax
import jax.numpy as jnp
from jax import lax
from jax.experimental import pallas as pl
from jax.experimental.pallas import tpu as pltpu
from jax.sharding import PartitionSpec as P

beta_one = 0.9
beta_two = 0.999
correct_one = 1.0 - 0.9**5
correct_two = 1.0 - 0.999**5
adam_eps = 1e-08
learn_rate = 0.05
weight_decay = 1.0
peak_eps = 1e-06

MIB = 1024 * 1024
LEVELS = 32000.0
PLACE_HINT = 1 << 30
TAIL = 16


def params(mib=24):
    return pltpu.CompilerParams(vmem_limit_bytes=mib * MIB)


def hint(amount):
    return pl.CostEstimate(flops=amount, bytes_accessed=amount, transcendentals=0)


def pick_kernel(strips, table_ref, x_ref, out_ref, buffer, sems_in, sems_out):
    rows = x_ref.shape[0]
    width = out_ref.shape[1]
    size = rows // strips
    moves = []
    for k in range(out_ref.shape[0] // size):
        i, j = divmod(k, strips)
        start = pl.multiple_of(table_ref[i] * width, width)
        there = pl.ds(k * size, size)
        moves.append(
            (
                pltpu.make_async_copy(
                    x_ref.at[pl.ds(j * size, size), pl.ds(start, width)],
                    buffer.at[there, :],
                    sems_in.at[k],
                ),
                pltpu.make_async_copy(buffer.at[there, :], out_ref.at[there, :], sems_out.at[k]),
            )
        )
    for come, _ in moves:
        come.start()
    for come, go in moves:
        come.wait()
        go.start()
    for _, go in moves:
        go.wait()


def pick_columns(x, chunks, width):
    rows, count, strips = x.shape[0], chunks.shape[0], 4
    anywhere = pl.BlockSpec(memory_space=pl.ANY)
    return pl.pallas_call(
        functools.partial(pick_kernel, strips),
        out_shape=jax.ShapeDtypeStruct((count * rows, width), x.dtype),
        in_specs=[pl.BlockSpec(memory_space=pltpu.SMEM), anywhere],
        out_specs=anywhere,
        scratch_shapes=[
            pltpu.VMEM((count * rows, width), x.dtype),
            pltpu.SemaphoreType.DMA((strips * count,)),
            pltpu.SemaphoreType.DMA((strips * count,)),
        ],
        compiler_params=params(60),
        cost_estimate=hint(1024),
        name="pick_columns",
    )(chunks, x)


def gate_kernel(*refs):
    pass


def gate(x, after, work=1024):
    if not after and work == 1024:
        return x
    anywhere = pl.BlockSpec(memory_space=pl.ANY)
    return pl.pallas_call(
        gate_kernel,
        out_shape=jax.ShapeDtypeStruct(x.shape, x.dtype),
        in_specs=[anywhere] * (1 + len(after)),
        out_specs=anywhere,
        input_output_aliases={0: 0},
        cost_estimate=hint(work),
        name="gate",
    )(x, *after)


def contract(rows_ref, hidden_ref):
    return lax.dot_general(
        rows_ref[...],
        hidden_ref[...],
        (((0,), (0,)), ((), ())),
        preferred_element_type=jnp.float32,
    )


def group_sum(count, refs):
    rows, hidden = refs[1 : count + 1], refs[count + 1 : 2 * count + 1]
    total = contract(rows[0], hidden[0])
    for k in range(1, count):
        total = total + contract(rows[k], hidden[k])
    return total


def encode(values, out):
    block = values.shape[0]
    top = jnp.maximum(jnp.max(jnp.abs(values), axis=0, keepdims=True), 1e-30)
    exponent = jnp.floor(jnp.log2(top)) + 1.0
    codes = jnp.round(values * (1.0 / (jnp.exp2(exponent) * (1.0 / LEVELS))))
    out[:block, :] = codes.astype(jnp.int32).astype(jnp.int16)
    out[block:, :] = jnp.broadcast_to(
        exponent.astype(jnp.int32), (TAIL, values.shape[1])
    ).astype(jnp.int16)


def decode(coded, rows):
    block = coded.shape[0] - TAIL
    exponent = coded[block : block + 1, :].astype(jnp.int32).astype(jnp.float32)
    codes = coded[rows, :].astype(jnp.int32).astype(jnp.float32)
    return codes * (jnp.exp2(exponent) * (1.0 / LEVELS))


def code_kernel(count, *refs):
    encode(group_sum(count, refs), refs[-1].at[0])


def sum_kernel(count, *refs):
    refs[-1][...] = group_sum(count, refs)


def summed(kernel, rows, order, hidden, at, width, block, out_shape, out_spec, name):
    count = len(hidden)
    depth, ffn = hidden[0].shape
    first = at // block
    return pl.pallas_call(
        functools.partial(kernel, count),
        out_shape=out_shape,
        grid_spec=pltpu.PrefetchScalarGridSpec(
            num_scalar_prefetch=1,
            grid=(width // block,),
            in_specs=[
                pl.BlockSpec(
                    (depth, block), functools.partial(lambda k, i, table: (table[k], first + i), k)
                )
                for k in range(count)
            ]
            + [pl.BlockSpec((depth, ffn), lambda i, table: (0, 0))] * count,
            out_specs=out_spec,
        ),
        compiler_params=params(),
        cost_estimate=hint(1024),
        name=name,
    )(order, *[rows] * count, *hidden)


def coded_sum(rows, order, hidden, at, width, block):
    ffn = hidden[0].shape[1]
    shape = jax.ShapeDtypeStruct((width // block, block + TAIL, ffn), jnp.int16)
    spec = pl.BlockSpec((1, block + TAIL, ffn), lambda i, table: (i, 0, 0))
    return summed(
        code_kernel, rows, order, hidden, at, width, block, shape, spec, "coded_sum"
    )


def own_sum(rows, order, hidden, block):
    ffn, width = hidden[0].shape[1], rows.shape[1]
    shape = jax.ShapeDtypeStruct((width, ffn), jnp.float32)
    spec = pl.BlockSpec((block, ffn), lambda i, table: (i, 0))
    return summed(sum_kernel, rows, order, hidden, 0, width, block, shape, spec, "own_sum")


def adam_kernel(arrays, at, block, size, ahead, *refs):
    streams = refs[:5]
    refs, (early,) = (refs[:-11] + refs[-10:], refs[-11:-10]) if ahead else (refs, (None,))
    outs, top_ref = refs[-14:-11], refs[-11]
    buffers, results = refs[-10:-5], refs[-5:-2]
    arrived, left = refs[-2:]
    own, coded, master, one, two = buffers
    steps = coded.shape[0] * block // size
    comes, leaves = [], []
    for i in range(steps):
        here, there = pl.ds(i * size, size), pl.ds(at + i * size, size)
        pairs = [(x.at[there, :], y.at[here, :]) for x, y in zip(streams[2:], buffers[2:])]
        pairs.append((streams[0].at[there, :], own.at[here, :]))
        if i * size % block == 0:
            b = i * size // block
            pairs.append((streams[1].at[b], coded.at[b]))
        comes.append(
            [pltpu.make_async_copy(x, y, arrived.at[i, k]) for k, (x, y) in enumerate(pairs)]
        )
        leaves.append(
            [
                pltpu.make_async_copy(y.at[here, :], x.at[there, :], left.at[i, k])
                for k, (x, y) in enumerate(zip(outs, results))
            ]
        )
    for copies in comes:
        for copy in copies:
            copy.start()
    highest = None
    for i in range(steps):
        for copy in comes[i]:
            copy.wait()
        here = pl.ds(i * size, size)
        b, off = i * size // block, i * size % block
        grad = own[here, :] + decode(coded.at[b], pl.ds(off, size))
        first = beta_one * one[here, :].astype(jnp.float32) + (1.0 - beta_one) * grad
        second = beta_two * two[here, :].astype(jnp.float32) + (1.0 - beta_two) * grad * grad
        update = (first * (1.0 / correct_one)) / (
            jnp.sqrt(second * (1.0 / correct_two)) + adam_eps
        )
        weight = master[here, :]
        new_master = weight - learn_rate * (update + weight_decay * weight)
        results[0][here, :] = new_master
        results[1][here, :] = first.astype(jnp.bfloat16)
        results[2][here, :] = second.astype(jnp.bfloat16)
        for copy in leaves[i]:
            copy.start()
        top = jnp.max(jnp.abs(new_master), axis=0, keepdims=True)
        highest = top if highest is None else jnp.maximum(highest, top)
        if ahead and off + size == block:
            encode(results[0][pl.ds(b * block, block), :], early.at[b])
    peak = jnp.max(highest)
    if arrays:
        peak = jnp.maximum(peak, refs[5 + arrays][0])
    top_ref[0] = peak
    for copies in leaves:
        for copy in copies:
            copy.wait()


def adam(own, coded, master, one, two, at, block, ahead, earlier=()):
    shard, ffn = master.shape
    size = min(64, block)
    width = coded.shape[0] * block
    steps = width // size
    anywhere = pl.BlockSpec(memory_space=pl.ANY)
    scalar = pl.BlockSpec(memory_space=pltpu.SMEM)
    arrays = max(len(earlier) - 1, 0)
    types = (jnp.float32, jnp.bfloat16, jnp.bfloat16)
    return pl.pallas_call(
        functools.partial(adam_kernel, arrays, at, block, size, ahead),
        out_shape=tuple(jax.ShapeDtypeStruct((shard, ffn), t) for t in types)
        + (jax.ShapeDtypeStruct((1,), jnp.float32),)
        + (jax.ShapeDtypeStruct(coded.shape, jnp.int16),) * ahead,
        in_specs=[anywhere] * (5 + arrays) + [scalar] * (arrays > 0),
        out_specs=(anywhere, anywhere, anywhere, scalar)
        + (pl.BlockSpec(memory_space=pltpu.VMEM),) * ahead,
        scratch_shapes=[pltpu.VMEM((width, ffn), jnp.float32), pltpu.VMEM(coded.shape, jnp.int16)]
        + [pltpu.VMEM((width, ffn), t) for t in types * 2]
        + [pltpu.SemaphoreType.DMA((steps, 5)), pltpu.SemaphoreType.DMA((steps, 3))],
        input_output_aliases={5 + k: k for k in range(arrays)},
        compiler_params=params(60),
        cost_estimate=hint(1024),
        name="adam",
    )(own, coded, master, one, two, *earlier)


def scale_kernel(peak_ref, weight_ref, *refs):
    out_ref = refs[-1]
    factor = 1.0 / (jnp.full((1, out_ref.shape[1]), peak_ref[0], jnp.float32) + peak_eps)
    out_ref[...] = (weight_ref[...] * factor).astype(jnp.bfloat16)


def scale(weight, peak, at, rows, after):
    ffn = weight.shape[1]
    block = rows // 2
    return pl.pallas_call(
        scale_kernel,
        out_shape=jax.ShapeDtypeStruct((rows, ffn), jnp.bfloat16),
        grid=(2,),
        in_specs=[
            pl.BlockSpec(memory_space=pltpu.SMEM),
            pl.BlockSpec((block, ffn), lambda i: (at // block + i, 0)),
        ]
        + [pl.BlockSpec(memory_space=pl.ANY)] * len(after),
        out_specs=pl.BlockSpec((block, ffn), lambda i: (i, 0)),
        compiler_params=params(),
        cost_estimate=hint(1024),
        name="scale",
    )(peak, weight, *after)


def place_kernel(strips, coded, table_ref, factor_ref, piece, *refs):
    whole, landed, scaled, sems_in, sems_out = refs[-5:]
    rows = scaled.shape[0]
    size = rows // strips
    at = pl.multiple_of(table_ref[0] * rows, rows)
    comes, leaves = [], []
    for j in range(strips):
        here = pl.ds(j * size, size)
        comes.append(
            pltpu.make_async_copy(piece.at[here, :], landed.at[here, :], sems_in.at[j])
        )
        leaves.append(
            pltpu.make_async_copy(
                (scaled if coded else landed).at[here, :],
                whole.at[pl.ds(at + j * size, size), :],
                sems_out.at[j],
            )
        )
    if coded:
        last = pl.ds(rows, TAIL)
        comes.append(
            pltpu.make_async_copy(piece.at[last, :], landed.at[last, :], sems_in.at[strips])
        )
    for copy in comes:
        copy.start()
    if coded:
        comes[-1].wait()
    for j in range(strips):
        comes[j].wait()
        if coded:
            here = pl.ds(j * size, size)
            values = decode(landed, here) * factor_ref[0]
            scaled[here, :] = values.astype(jnp.bfloat16)
        leaves[j].start()
    for copy in leaves:
        copy.wait()


def place(whole, shape, piece, spot, factor):
    coded = piece.dtype == jnp.int16
    rows, ffn = piece.shape
    rows -= TAIL * coded
    strips = 4
    anywhere = pl.BlockSpec(memory_space=pl.ANY)
    scalars = pl.BlockSpec(memory_space=pltpu.SMEM)
    earlier = () if whole is None else (whole,)
    return pl.pallas_call(
        functools.partial(place_kernel, strips, coded),
        out_shape=jax.ShapeDtypeStruct(shape, jnp.bfloat16),
        in_specs=[scalars, scalars, anywhere] + [anywhere] * len(earlier),
        out_specs=anywhere,
        scratch_shapes=[
            pltpu.VMEM(piece.shape, piece.dtype),
            pltpu.VMEM((rows, ffn), jnp.bfloat16),
            pltpu.SemaphoreType.DMA((strips + 1,)),
            pltpu.SemaphoreType.DMA((strips,)),
        ],
        input_output_aliases={3: 0} if earlier else {},
        compiler_params=params(),
        cost_estimate=hint(PLACE_HINT),
        name="place",
    )(spot.astype(jnp.int32).reshape(1), factor, piece, *earlier)


def local(out_grad, hidden_saved, recv_counts, master_weight, moment_one, moment_two):
    experts = lax.axis_size("expert")
    half = lax.axis_size("near")
    replicas = lax.axis_size("far") * half
    near, far = lax.axis_index("near"), lax.axis_index("far")
    me = far * half + near
    capacity = out_grad.shape[0] // experts
    shard, ffn = master_weight.shape
    block, part = min(256, shard // 2), shard // 2
    chain = ("far", "near")

    def swap(x, k):
        return lax.ppermute(x, chain, [(i, i ^ k) for i in range(replicas)])

    live = (jnp.arange(capacity)[None, :] < recv_counts[:, None]).reshape(-1)
    hidden = jnp.where(live[:, None], hidden_saved, jnp.zeros((), jnp.bfloat16))
    hiddens = [hidden] + [gate(swap(hidden, k), (), 1 << 35) for k in range(1, half)]
    order = jnp.stack([near ^ k for k in range(half)]).astype(jnp.int32)

    def arrive(side, at, width, after):
        chunks = ((side * half + jnp.arange(half)) * shard + at) // width
        picked = gate(pick_columns(out_grad, chunks.astype(jnp.int32), width), after)
        return lax.all_to_all(picked, ("near", "expert"), 0, 0, tiled=True)

    got = arrive(1 - far, 0, shard, ())
    partials = [
        coded_sum(got, order, hiddens, at, block, block) for at in range(0, shard, block)
    ]
    coded = [swap(partial, half) for partial in partials]
    coded[0] = gate(coded[0], (), 1 << 35)

    got = arrive(far, 0, shard, (partials[0],))
    own = own_sum(got, order, hiddens, block)
    results, ahead = (), []
    for p, codes in enumerate(coded):
        early = p * block < part
        results = adam(
            own,
            codes,
            master_weight,
            moment_one,
            moment_two,
            p * block,
            block,
            early,
            tuple(results),
        )
        if early:
            *results, piece = results
            ahead.append(piece[0])
    new_master, new_one, new_two, peak = results

    beside = [gate(swap(piece, 1), (), work) for piece, work in zip(ahead, (1<<34, 1024))]
    step = 1
    while step < replicas:
        peak = jnp.maximum(peak, swap(peak, step))
        step *= 2
    late = scale(new_master, peak, part, part, beside)
    factor = 1.0 / (peak + peak_eps)

    def spread(piece, next_to=None):
        held, distance = [(piece, me)], half
        while distance:
            for x, source in list(held):
                if next_to is not None and distance == 1 and x is piece:
                    got = next_to
                else:
                    got = swap(x, distance)
                held.append((got, source ^ distance))
            distance //= 2
        return held

    last = spread(late)
    flows = [(part, last)]
    for p, piece in enumerate(ahead):
        flows.append((p * block, spread(gate(piece, (last[1][0],)), beside[p])))
    last[0] = (gate(late, (flows[1][1][1][0],)), me)
    whole_shape = (replicas * shard, ffn)
    scaled = None
    for i in range(replicas):
        for at, held in flows:
            got, source = held[i]
            rows = part if at == part else block
            spot = (source * shard + at) // rows
            scaled = place(scaled, whole_shape, got, spot, factor)
    return new_master, new_one, new_two, scaled, peak


def solution(mesh):
    experts, replicas = mesh.devices.shape
    cut = jax.sharding.Mesh(
        mesh.devices.reshape(experts, 2, replicas // 2), ("expert", "far", "near")
    )
    everything = ("expert", "far", "near")
    placed = P(everything, None)
    return jax.shard_map(
        local,
        mesh=cut,
        in_specs=(placed, placed, P(everything), placed, placed, placed),
        out_specs=(placed, placed, placed, P("expert", None), P("expert")),
        check_vma=False,
    )
```
